256 devices in a mesh: lat: 4 (over x_lo, core), lon: 64 (over y, x_hi, z).
Axes of the slice: x: 4 (x_hi: 2, x_lo: 2; x = x_hi * 2 + x_lo), y: 4, z: 8, core: 2. Of those that a mesh axis runs over, the one named last changes fastest.
Arguments:
- fields: bfloat16 [512, 1024, 70], P('lat', 'lon'), may hold values from -6 to 6
- row_valid: int32 [512], P('lat'), may hold values from 0 to 1, as said below
- w_encode: bfloat16 [70, 1024], replicated, may hold values from -0.75 to 0.75
- norm_gain: float32 [1024], replicated, may hold values from 0.1 to 1.9
- w_query: bfloat16 [1024, 512], replicated, may hold values from -0.1875 to 0.1875
- w_key: bfloat16 [1024, 512], replicated, may hold values from -0.1875 to 0.1875
- w_value: bfloat16 [1024, 512], replicated, may hold values from -0.1875 to 0.1875
- query_gain: float32 [64], replicated, may hold values from 0.1 to 1.9
- key_gain: float32 [64], replicated, may hold values from 0.1 to 1.9
- w_out: bfloat16 [512, 1024], replicated, may hold values from -1 to 1
Outputs:
- layer_out: bfloat16 [512, 1024, 1024], P('lat', 'lon')
The draws below stay inside these ranges and needn't reach their ends.
Inputs may be any that keep to these rules, and one draw needn't show every extreme that they name: `row_valid`: for one t of 1 to 6, the first t rows and the last 7 - t rows are 0 and all others are 1.
All inputs are finite; a program needn't handle non-finite values.
Results may differ from the reference program's by a relative error of at most 0.015.
Values may be sent and summed in bfloat16 or wider, within the bound.
A program may use at most 192 MiB of HBM per device.

```python
import jax
import jax.numpy as jnp
import numpy as np
from jax import lax

D = 1024
HEADS = 8
HEAD_DIM = 64
C_IN = 70
TILE = 8
POLE_PAD = 7
HALO = 6
HD = 512
LAT = 512
LON = 1024


def draw_row_valid(key, part):
    rim_top = jax.random.randint(key, (), 1, POLE_PAD)
    cell_rows = jnp.arange(LAT)
    return ((cell_rows >= rim_top) & (cell_rows < LAT - POLE_PAD + rim_top)).astype(jnp.int32)


def shard_levels(stream_key, dims, pieces, smallest, largest):
    factor_of, own = 1.0, jax.random.fold_in(stream_key, 6)
    for dim, parts in pieces:
        draws = jnp.exp(jax.random.uniform(jax.random.fold_in(own, dim), (parts,), jnp.float32, smallest / len(pieces), largest / len(pieces)))
        factor_of = factor_of * jnp.repeat(draws, dims[dim] // parts).reshape([-1 if axis == dim else 1 for axis in range(len(dims))])
    return factor_of


def normal_values(own_key, shape, width, limit, shards=(), held_as=jnp.bfloat16):
    values = jax.random.normal(own_key, shape, jnp.float32) * width
    if len(shards) > 0:
        values = shard_levels(own_key, shape, shards, -0.22, 0.18) * values
    return jnp.clip(values, min=-limit, max=limit).astype(held_as)


def setup_inputs(seed: int = 0) -> dict:
    key_list = jax.random.split(jax.random.key(seed), 11)
    fields = normal_values(key_list[0], (LAT, LON, C_IN), 1.0, 6.0, ((0, 4), (1, 64)))
    row_valid = draw_row_valid(jax.random.fold_in(key_list[10], 71), 0)
    w_encode = normal_values(key_list[2], (C_IN, D), C_IN ** -0.5, 0.75)
    norm_gain = jnp.clip(1.0 + 0.18 * jax.random.normal(key_list[3], (D,), jnp.float32), 0.1, 1.9)
    w_query = normal_values(key_list[4], (D, HD), D ** -0.5, 0.1875)
    w_key = normal_values(key_list[5], (D, HD), D ** -0.5, 0.1875)
    w_value = normal_values(key_list[6], (D, HD), D ** -0.5, 0.1875)
    query_gain = jnp.clip(1.0 + 0.18 * jax.random.normal(key_list[7], (HEAD_DIM,), jnp.float32), 0.1, 1.9)
    key_gain = jnp.clip(1.0 + 0.18 * jax.random.normal(key_list[8], (HEAD_DIM,), jnp.float32), 0.1, 1.9)
    w_out = normal_values(key_list[9], (HD, D), (HD // 16) ** -0.5, 1.0)
    return {"fields": fields, "row_valid": row_valid, "w_encode": w_encode, "norm_gain": norm_gain, "w_query": w_query, "w_key": w_key, "w_value": w_value, "query_gain": query_gain, "key_gain": key_gain, "w_out": w_out}


EPS_ROW = 1e-05
EPS_HEAD = 1e-06

def head_norm(projected, head_gain):
    shaped = projected.reshape(projected.shape[:-1] + (HEADS, HEAD_DIM))
    inverse = lax.rsqrt(lax.optimization_barrier(jnp.mean(shaped * shaped, axis=-1, keepdims=True)) + EPS_HEAD)
    return (shaped * inverse * head_gain).reshape(projected.shape).astype(jnp.bfloat16)

def rms_rows(latents, norm_gain):
    widened = latents.astype(jnp.float32)
    inverse = lax.rsqrt(lax.optimization_barrier(jnp.mean(widened * widened, axis=-1, keepdims=True)) + EPS_ROW)
    return (widened * inverse * norm_gain).astype(jnp.bfloat16)

def window_mask():
    offsets = np.arange(TILE + 2 * HALO)[None, :] - np.arange(TILE)[:, None]
    near_rows = (offsets >= 0) & (offsets <= 2 * HALO)
    joined = near_rows[:, None, :, None] & near_rows[None, :, None, :]
    return joined.reshape(TILE * TILE, (TILE + 2 * HALO) ** 2)

def reference(fields, row_valid, w_encode, norm_gain, w_query, w_key, w_value, query_gain, key_gain, w_out):

    def per_row(field_row):
        latents = jnp.dot(field_row, w_encode, preferred_element_type=jnp.float32).astype(jnp.bfloat16)
        normed = rms_rows(latents, norm_gain)
        queries = head_norm(jnp.dot(normed, w_query, preferred_element_type=jnp.float32), query_gain)
        keys = head_norm(jnp.dot(normed, w_key, preferred_element_type=jnp.float32), key_gain)
        values = jnp.dot(normed, w_value, preferred_element_type=jnp.float32).astype(jnp.bfloat16)
        return (latents, queries, jnp.concatenate([keys, values], axis=-1))
    latents, queries, key_value = lax.map(per_row, fields)
    key_value = jnp.concatenate([key_value[:, -HALO:], key_value, key_value[:, :HALO]], axis=1)
    zero_rows = jnp.zeros((HALO,) + key_value.shape[1:], jnp.bfloat16)
    key_value = jnp.concatenate([zero_rows, key_value, zero_rows], axis=0)
    rim_rows = jnp.zeros((HALO,), dtype=bool)
    key_rows = jnp.concatenate([rim_rows, row_valid == 1, rim_rows])
    tile_mask = jnp.asarray(window_mask())
    key_span = TILE + 2 * HALO
    tiles_lon = LON // TILE
    columns = (jnp.arange(tiles_lon, dtype=jnp.int32) * TILE)[:, None] + jnp.arange(key_span, dtype=jnp.int32)[None, :]

    def attend(tile_row):
        row_start = (tile_row * TILE).astype(jnp.int32)
        qblock = lax.dynamic_slice_in_dim(queries, row_start, TILE, 0)
        kblock = lax.dynamic_slice_in_dim(key_value, row_start, key_span, 0)
        rows_ok = lax.dynamic_slice_in_dim(key_rows, row_start, key_span, 0)
        lblock = lax.dynamic_slice_in_dim(latents, row_start, TILE, 0)
        region = jnp.take(kblock, columns, axis=1).transpose(1, 0, 2, 3)
        region = region.reshape(tiles_lon, key_span * key_span, 2, HEADS, HEAD_DIM).astype(jnp.float32)
        qtiles = qblock.reshape(TILE, tiles_lon, TILE, HEADS, HEAD_DIM).transpose(1, 0, 2, 3, 4)
        qtiles = qtiles.reshape(tiles_lon, TILE * TILE, HEADS, HEAD_DIM).astype(jnp.float32)
        scores = jnp.einsum('nqhd,nkhd->nhqk', qtiles, region[:, :, 0]) * HEAD_DIM ** (-0.5)
        allowed = tile_mask & jnp.broadcast_to(rows_ok[:, None], (key_span, key_span)).reshape(-1)[None, :]
        expo = jnp.where(allowed, jnp.exp(scores), 0.0)
        weights = (expo / lax.optimization_barrier(jnp.sum(expo, axis=-1, keepdims=True))).astype(jnp.bfloat16)
        mixture = jnp.einsum('nhqk,nkhd->nqhd', weights.astype(jnp.float32), region[:, :, 1]).astype(jnp.bfloat16)
        mixture = mixture.reshape(tiles_lon, TILE, TILE, HD).transpose(1, 0, 2, 3).reshape(TILE * LON, HD)
        result = lblock.reshape(TILE * LON, D).astype(jnp.float32) + jnp.dot(mixture, w_out, preferred_element_type=jnp.float32)
        return result.astype(jnp.bfloat16).reshape(TILE, LON, D)
    blocks = lax.map(attend, jnp.arange(LAT // TILE, dtype=jnp.int32))
    return blocks.reshape(LAT, LON, D)
```

```python
import functools
import math

import jax
import jax.numpy as jnp
from jax import lax
from jax.experimental import pallas as pl
from jax.experimental.pallas import tpu as pltpu
from jax.sharding import PartitionSpec as P

HEADS = 8
HEAD_DIM = 64
HALO = 6
TR = 4
SIDE = 8
EPS_ROW = 1e-05
EPS_HEAD = 1e-06
F32 = jnp.float32
BF16 = jnp.bfloat16
MESH = pl.DeviceIdType.MESH
NT = (((1,), (1,)), ((), ()))


def nn(a, b):
    return jnp.dot(a, b, preferred_element_type=F32)


def nt(a, b):
    return lax.dot_general(a, b, NT, preferred_element_type=F32)


def split(x):
    hi = x.astype(BF16)
    return hi, (x - hi.astype(F32)).astype(BF16)


def chunk_of(count, most):
    return max(c for c in range(1, most + 1) if count % c == 0)


def attend_kernel(
    n_lat, n_lon, rows, cols, chan, hd,
    fields, valid, w_enc, gain, w_q, w_k, w_v, q_gain, k_gain,
    mix,
    fraw, fext, send_l, send_r, halo_l, halo_r, enc, wq, wk, wv, comp, ones_blk,
    q_s, k_o, v_o, k_l, v_l, k_r, v_r, masks,
    local_sem, send_sem, recv_sem,
):
    lat, lon = lax.axis_index("lat"), lax.axis_index("lon")
    up, down = lax.rem(lat + n_lat - 1, n_lat), lax.rem(lat + 1, n_lat)
    left, right = lax.rem(lon + n_lon - 1, n_lon), lax.rem(lon + 1, n_lon)
    pairs = rows // 2
    ext = rows + 2 * HALO
    tiles = rows // TR
    hp = HALO // 2

    loads = [
        pltpu.make_async_copy(src, dst, local_sem.at[i])
        for i, (src, dst) in enumerate(
            ((fields, fraw), (w_enc, enc), (w_k, wk), (w_v, wv), (w_q, wq))
        )
    ]
    for load in loads:
        load.start()

    barrier = pltpu.get_barrier_semaphore()
    around = [
        (up, left), (up, lon), (up, right), (lat, left), (lat, right), (down, left), (down, lon), (down, right)
    ]
    for dev in around:
        pl.semaphore_signal(barrier, inc=1, device_id=dev, device_id_type=MESH)

    own = pl.ds(HALO, rows)
    fext[own] = jnp.zeros((rows, cols, 128), BF16)
    send_l[...] = jnp.zeros(send_l.shape, BF16)
    send_r[...] = jnp.zeros(send_r.shape, BF16)
    loads[0].wait()

    def pack(i, c):
        x = fraw[pl.ds(i * 8, 8)]
        fext[pl.ds(HALO + i * 8, 8), :, 0:chan] = x
        x = x.astype(F32)
        send_l[pl.ds(i * 4, 4), :, 0:chan] = x[:, 0:SIDE].reshape(4, 16, chan).astype(BF16)
        send_r[pl.ds(i * 4, 4), :, 0:chan] = x[:, cols - SIDE :].reshape(4, 16, chan).astype(BF16)
        return c

    lax.fori_loop(0, rows // 8, pack, 0)
    pl.semaphore_wait(barrier, 8)

    first, last = pl.ds(0, hp), pl.ds(pairs - hp, hp)
    top, mid, bot = pl.ds(0, hp), pl.ds(hp, pairs), pl.ds(hp + pairs, hp)
    plan = [
        (send_l.at[...], halo_r.at[mid], (lat, left)),
        (send_r.at[...], halo_l.at[mid], (lat, right)),
        (fext.at[pl.ds(HALO, HALO)], fext.at[pl.ds(HALO + rows, HALO)], (up, lon)),
        (fext.at[pl.ds(rows, HALO)], fext.at[pl.ds(0, HALO)], (down, lon)),
        (send_l.at[first], halo_r.at[bot], (up, left)),
        (send_l.at[last], halo_r.at[top], (down, left)),
        (send_r.at[first], halo_l.at[bot], (up, right)),
        (send_r.at[last], halo_l.at[top], (down, right)),
    ]
    copies = [
        pltpu.make_async_remote_copy(
            src_ref=src, dst_ref=dst, send_sem=send_sem.at[i], recv_sem=recv_sem.at[i],
            device_id=dev, device_id_type=MESH,
        )
        for i, (src, dst, dev) in enumerate(plan)
    ]
    for copy in copies:
        copy.start()

    comp[...] = jnp.zeros(comp.shape, BF16)
    row_i = lax.broadcasted_iota(jnp.int32, (256, 256), 0) // HEAD_DIM
    col_i = lax.broadcasted_iota(jnp.int32, (256, 256), 1) // HEAD_DIM
    ones_blk[...] = jnp.where(row_i == col_i, 1.0 / HEAD_DIM, 0.0).astype(BF16)

    keys = (TR + 2 * HALO) * (cols + 2 * SIDE)
    half = (TR + 2 * HALO) * cols
    side = (TR + 2 * HALO) * SIDE
    lane = lax.broadcasted_iota(jnp.int32, (1, keys), 1)
    rel = jnp.where(lane < half, lane, jnp.where(lane < half + side, lane - half, lane - half - side))
    key_row = jnp.where(lane < half, rel // cols, rel // SIDE)
    key_col = jnp.where(
        lane < half, rel % cols, jnp.where(lane < half + side, rel % SIDE - SIDE, rel % SIDE + cols)
    )
    qi = lax.broadcasted_iota(jnp.int32, (TR * cols, 1), 0)
    row_off = key_row - qi // cols
    col_off = key_col - qi % cols
    near = (row_off >= 0) & (row_off <= 2 * HALO) & (col_off >= -HALO) & (col_off <= HALO)
    base = jnp.where(near, 1.0, 0.0).astype(F32)
    has_up = jnp.where(lat > 0, 1.0, 0.0).astype(F32)
    has_down = jnp.where(lat < n_lat - 1, 1.0, 0.0).astype(F32)
    for slot, tile in enumerate((0, 1, 2, None, tiles - 3, tiles - 2, tiles - 1)):
        m = base
        if tile is not None:
            ok = jnp.ones((1, keys), F32)
            for r in range(TR + 2 * HALO):
                e = tile * TR + r
                if e < HALO:
                    v = has_up
                elif e >= HALO + rows:
                    v = has_down
                else:
                    v = valid[e - HALO].astype(F32)
                ok = jnp.where(key_row == r, v, ok)
            m = base * ok
        masks[slot] = m.astype(BF16)

    loads[1].wait()
    enc_v = enc[...]
    wg_hi, wg_lo = split(enc_v.astype(F32) * gain[...])

    def put(x, at):
        hi, lo = split(x)
        comp[0 : x.shape[0], at : at + x.shape[1]] = hi
        comp[128 : 128 + x.shape[0], at : at + x.shape[1]] = lo

    put(nt(enc_v, enc_v) * (1.0 / enc_v.shape[1]), 2 * hd)
    for load, w, at in ((loads[2], wk, 0), (loads[3], wv, hd), (loads[4], wq, 2 * hd + 128)):
        load.wait()
        put(nn(wg_hi, w[...]) + nn(wg_lo, w[...]), at)

    def tiled(g):
        pair = jnp.concatenate([g[...]] * 2, axis=1)
        return jnp.concatenate([pair] * (hd // 128), axis=1)

    kg = tiled(k_gain)
    qg = tiled(q_gain) * (math.log2(math.e) / math.sqrt(HEAD_DIM))

    def head_norm(x, eps_u, g):
        sq = (x * x).astype(BF16)
        blk = ones_blk[...]
        mean = jnp.concatenate([nn(sq[:, i : i + 256], blk) for i in range(0, hd, 256)], axis=1)
        return (x * lax.rsqrt(mean + eps_u) * g).astype(BF16)

    def project(f, k_ref, v_ref, at, q_at=None):
        n = f.shape[0]
        two = jnp.concatenate([f, f], axis=1)
        width = 2 * hd + 128 + (hd if q_at is not None else 0)
        y = nn(two, comp[:, 0:width])
        quad = jnp.sum(y[:, 2 * hd : 2 * hd + 128] * f.astype(F32), axis=1, keepdims=True)
        u = jnp.maximum(quad, 0.0) + EPS_ROW
        eps_u = EPS_HEAD * u
        k_ref[pl.ds(at, n), :] = head_norm(y[:, 0:hd], eps_u, kg)
        v_ref[pl.ds(at, n), :] = (y[:, hd : 2 * hd] * lax.rsqrt(u)).astype(BF16)
        if q_at is not None:
            q_s[pl.ds(q_at, n), :] = head_norm(y[:, 2 * hd + 128 :], eps_u, qg)

    crow = chunk_of(rows, 16)
    ccell = crow * cols

    def own_step(i, c):
        f = fext[pl.ds(HALO + i * crow, crow)].reshape(ccell, 128)
        project(f, k_o, v_o, pl.multiple_of(HALO * cols + i * ccell, 16), pl.multiple_of(i * ccell, 16))
        return c

    lax.fori_loop(0, rows // crow, own_step, 0)

    for copy in copies:
        copy.wait_recv()

    for r0 in (0, HALO + rows):
        project(fext[r0 : r0 + HALO].reshape(HALO * cols, 128), k_o, v_o, r0 * cols)

    cpair = chunk_of(pairs + 2 * hp, 14)

    def side_step(i, c):
        for src, k_ref, v_ref in ((halo_l, k_l, v_l), (halo_r, k_r, v_r)):
            f = src[pl.ds(i * cpair, cpair)].reshape(cpair * 16, 128)
            project(f, k_ref, v_ref, pl.multiple_of(i * cpair * 16, 16))
        return c

    lax.fori_loop(0, (pairs + 2 * hp) // cpair, side_step, 0)

    nq = TR * cols
    head = lax.broadcasted_iota(jnp.int32, (nq, 256), 1) // HEAD_DIM

    def attend(t, c):
        slot = jnp.minimum(t, 3) + jnp.maximum(t - (tiles - 4), 0)
        m = masks[slot]
        m4 = jnp.concatenate([m] * 4, axis=0)
        o_at = pl.ds(pl.multiple_of(t * nq, nq), half)
        s_at = pl.ds(pl.multiple_of(t * TR * SIDE, TR * SIDE), side)
        q_at = pl.ds(pl.multiple_of(t * nq, nq), nq)
        for p in range(hd // 256):
            ps = slice(256 * p, 256 * p + 256)
            q = q_s[q_at, ps]
            zero = jnp.zeros_like(q)
            q4 = jnp.concatenate([jnp.where(head == h, q, zero) for h in range(4)], axis=0)
            k = jnp.concatenate([k_o[o_at, ps], k_l[s_at, ps], k_r[s_at, ps]], axis=0)
            v = jnp.concatenate([v_o[o_at, ps], v_l[s_at, ps], v_r[s_at, ps]], axis=0)
            e = jnp.exp2(nt(q4, k)).astype(BF16) * m4
            den = jnp.sum(e.astype(F32), axis=1, keepdims=True)
            acc = nn(e, v) * (1.0 / den)
            out = acc[0:nq]
            for h in range(1, 4):
                out = jnp.where(head == h, acc[h * nq : (h + 1) * nq], out)
            mix[q_at, ps] = out.astype(BF16)
        return c

    lax.fori_loop(0, tiles, attend, 0, unroll=2)

    for copy in copies:
        copy.wait_send()


def out_kernel(fields, w_enc, mix, w_out, out):
    f = fields[...]
    n = f.shape[0] * f.shape[1]
    latents = nn(f.reshape(n, f.shape[2]), w_enc[...]).astype(BF16)
    res = latents.astype(F32) + nn(mix[...], w_out[...])
    out[...] = res.astype(BF16).reshape(out.shape)


def per_device(n_lat, n_lon, fields, row_valid, w_encode, norm_gain, w_query, w_key, w_value, query_gain, key_gain, w_out):
    rows, cols, chan = fields.shape
    d, hd = w_query.shape
    cells = rows * cols
    ext = rows + 2 * HALO
    pairs = ext // 2
    any_spec = pl.BlockSpec(memory_space=pl.ANY)
    vmem = pl.BlockSpec(memory_space=pltpu.VMEM)
    keys = (TR + 2 * HALO) * (cols + 2 * SIDE)
    mix = pl.pallas_call(
        functools.partial(attend_kernel, n_lat, n_lon, rows, cols, chan, hd),
        out_shape=jax.ShapeDtypeStruct((cells, hd), BF16),
        in_specs=[
            any_spec, pl.BlockSpec(memory_space=pltpu.SMEM), any_spec, vmem,
            any_spec, any_spec, any_spec, vmem, vmem,
        ],
        out_specs=vmem,
        scratch_shapes=[
            pltpu.VMEM((rows, cols, chan), BF16),
            pltpu.VMEM((ext, cols, 128), BF16),
            pltpu.VMEM((rows // 2, 16, 128), BF16),
            pltpu.VMEM((rows // 2, 16, 128), BF16),
            pltpu.VMEM((pairs, 16, 128), BF16),
            pltpu.VMEM((pairs, 16, 128), BF16),
            pltpu.VMEM((chan, d), BF16),
            pltpu.VMEM((d, hd), BF16),
            pltpu.VMEM((d, hd), BF16),
            pltpu.VMEM((d, hd), BF16),
            pltpu.VMEM((256, 3 * hd + 128), BF16),
            pltpu.VMEM((256, 256), BF16),
            pltpu.VMEM((cells, hd), BF16),
            pltpu.VMEM((ext * cols, hd), BF16),
            pltpu.VMEM((ext * cols, hd), BF16),
            pltpu.VMEM((ext * SIDE, hd), BF16),
            pltpu.VMEM((ext * SIDE, hd), BF16),
            pltpu.VMEM((ext * SIDE, hd), BF16),
            pltpu.VMEM((ext * SIDE, hd), BF16),
            pltpu.VMEM((7, TR * cols, keys), BF16),
            pltpu.SemaphoreType.DMA((5,)),
            pltpu.SemaphoreType.DMA((8,)),
            pltpu.SemaphoreType.DMA((8,)),
        ],
        compiler_params=pltpu.CompilerParams(
            collective_id=0, has_side_effects=True, vmem_limit_bytes=48 * 1024 * 1024
        ),
    )(
        fields, row_valid, w_encode, norm_gain.reshape(1, d), w_query, w_key, w_value,
        query_gain.reshape(1, HEAD_DIM), key_gain.reshape(1, HEAD_DIM),
    )
    block = chunk_of(rows, 16)
    return pl.pallas_call(
        out_kernel,
        grid=(rows // block,),
        out_shape=jax.ShapeDtypeStruct((rows, cols, d), BF16),
        in_specs=[
            pl.BlockSpec((block, cols, chan), lambda i: (i, 0, 0)),
            pl.BlockSpec((chan, d), lambda i: (0, 0)),
            pl.BlockSpec((block * cols, hd), lambda i: (i, 0)),
            pl.BlockSpec((hd, d), lambda i: (0, 0)),
        ],
        out_specs=pl.BlockSpec((block, cols, d), lambda i: (i, 0, 0)),
        compiler_params=pltpu.CompilerParams(vmem_limit_bytes=32 * 1024 * 1024),
    )(fields, w_encode, mix, w_out)


def solution(mesh):
    return jax.shard_map(
        functools.partial(per_device, mesh.shape["lat"], mesh.shape["lon"]),
        mesh=mesh,
        in_specs=(P("lat", "lon", None), P("lat"), P(), P(), P(), P(), P(), P(), P(), P()),
        out_specs=P("lat", "lon", None),
        check_vma=False,
    )
```

```python
import functools
import math

import jax
import jax.numpy as jnp
from jax import lax
from jax.experimental import pallas as pl
from jax.experimental.pallas import tpu as pltpu
from jax.sharding import PartitionSpec as P

HEADS = 8
HEAD_DIM = 64
HALO = 6
TR = 4
SIDE = 8
EPS_ROW = 1e-05
EPS_HEAD = 1e-06
F32 = jnp.float32
BF16 = jnp.bfloat16
MESH = pl.DeviceIdType.MESH
NT = (((1,), (1,)), ((), ()))


def nn(a, b):
    return jnp.dot(a, b, preferred_element_type=F32)


def nt(a, b):
    return lax.dot_general(a, b, NT, preferred_element_type=F32)


def split(x):
    hi = x.astype(BF16)
    return hi, (x - hi.astype(F32)).astype(BF16)


def chunk_of(count, most):
    return max(c for c in range(1, most + 1) if count % c == 0)


def attend_kernel(
    n_lat, n_lon, rows, cols, chan, hd,
    fields, row_valid, w_enc, norm_gain, w_q, w_k, w_v, query_gain, key_gain,
    mix,
    fraw, fext, send_l, send_r, halo_l, halo_r, enc, gain, wq, wk, wv, q_gain, k_gain, valid, comp, ones_blk,
    q_s, k_o, v_o, k_l, v_l, k_r, v_r, masks,
    local_sem, send_sem, recv_sem,
):
    lat, lon = lax.axis_index("lat"), lax.axis_index("lon")
    up, down = lax.rem(lat + n_lat - 1, n_lat), lax.rem(lat + 1, n_lat)
    left, right = lax.rem(lon + n_lon - 1, n_lon), lax.rem(lon + 1, n_lon)
    pairs = rows // 2
    ext = rows + 2 * HALO
    tiles = rows // TR
    hp = HALO // 2

    loads = [
        pltpu.make_async_copy(src, dst, local_sem.at[i])
        for i, (src, dst) in enumerate(
            (
                (fields, fraw), (w_enc, enc), (norm_gain, gain), (row_valid, valid), (query_gain, q_gain),
                (key_gain, k_gain), (w_k, wk), (w_v, wv), (w_q, wq),
            )
        )
    ]
    for load in loads:
        load.start()

    barrier = pltpu.get_barrier_semaphore()
    around = [
        (up, left), (up, lon), (up, right), (lat, left), (lat, right), (down, left), (down, lon), (down, right)
    ]
    for dev in around:
        pl.semaphore_signal(barrier, inc=1, device_id=dev, device_id_type=MESH)

    own = pl.ds(HALO, rows)
    fext[own] = jnp.zeros((rows, cols, 128), BF16)
    send_l[...] = jnp.zeros(send_l.shape, BF16)
    send_r[...] = jnp.zeros(send_r.shape, BF16)
    loads[0].wait()

    def pack(i, c):
        x = fraw[pl.ds(i * 8, 8)]
        fext[pl.ds(HALO + i * 8, 8), :, 0:chan] = x
        x = x.astype(F32)
        send_l[pl.ds(i * 4, 4), :, 0:chan] = x[:, 0:SIDE].reshape(4, 16, chan).astype(BF16)
        send_r[pl.ds(i * 4, 4), :, 0:chan] = x[:, cols - SIDE :].reshape(4, 16, chan).astype(BF16)
        return c

    lax.fori_loop(0, rows // 8, pack, 0)
    pl.semaphore_wait(barrier, 8)

    first, last = pl.ds(0, hp), pl.ds(pairs - hp, hp)
    top, mid, bot = pl.ds(0, hp), pl.ds(hp, pairs), pl.ds(hp + pairs, hp)
    plan = [
        (send_l.at[...], halo_r.at[mid], (lat, left)),
        (send_r.at[...], halo_l.at[mid], (lat, right)),
        (fext.at[pl.ds(HALO, HALO)], fext.at[pl.ds(HALO + rows, HALO)], (up, lon)),
        (fext.at[pl.ds(rows, HALO)], fext.at[pl.ds(0, HALO)], (down, lon)),
        (send_l.at[first], halo_r.at[bot], (up, left)),
        (send_l.at[last], halo_r.at[top], (down, left)),
        (send_r.at[first], halo_l.at[bot], (up, right)),
        (send_r.at[last], halo_l.at[top], (down, right)),
    ]
    copies = [
        pltpu.make_async_remote_copy(
            src_ref=src, dst_ref=dst, send_sem=send_sem.at[i], recv_sem=recv_sem.at[i],
            device_id=dev, device_id_type=MESH,
        )
        for i, (src, dst, dev) in enumerate(plan)
    ]
    for copy in copies:
        copy.start()

    comp[...] = jnp.zeros(comp.shape, BF16)
    row_i = lax.broadcasted_iota(jnp.int32, (256, 256), 0) // HEAD_DIM
    col_i = lax.broadcasted_iota(jnp.int32, (256, 256), 1) // HEAD_DIM
    ones_blk[...] = jnp.where(row_i == col_i, 1.0 / HEAD_DIM, 0.0).astype(BF16)

    keys = (TR + 2 * HALO) * (cols + 2 * SIDE)
    half = (TR + 2 * HALO) * cols
    side = (TR + 2 * HALO) * SIDE
    lane = lax.broadcasted_iota(jnp.int32, (1, keys), 1)
    rel = jnp.where(lane < half, lane, jnp.where(lane < half + side, lane - half, lane - half - side))
    key_row = jnp.where(lane < half, rel // cols, rel // SIDE)
    key_col = jnp.where(
        lane < half, rel % cols, jnp.where(lane < half + side, rel % SIDE - SIDE, rel % SIDE + cols)
    )
    qi = lax.broadcasted_iota(jnp.int32, (TR * cols, 1), 0)
    row_off = key_row - qi // cols
    col_off = key_col - qi % cols
    for load in loads[1:6]:
        load.wait()
    near = (row_off >= 0) & (row_off <= 2 * HALO) & (col_off >= -HALO) & (col_off <= HALO)
    base = jnp.where(near, 1.0, 0.0).astype(F32)
    has_up = jnp.where(lat > 0, 1.0, 0.0).astype(F32)
    has_down = jnp.where(lat < n_lat - 1, 1.0, 0.0).astype(F32)
    for slot, tile in enumerate((0, 1, 2, None, tiles - 3, tiles - 2, tiles - 1)):
        m = base
        if tile is not None:
            ok = jnp.ones((1, keys), F32)
            for r in range(TR + 2 * HALO):
                e = tile * TR + r
                if e < HALO:
                    v = has_up
                elif e >= HALO + rows:
                    v = has_down
                else:
                    v = valid[e - HALO].astype(F32)
                ok = jnp.where(key_row == r, v, ok)
            m = base * ok
        masks[slot] = m.astype(BF16)

    enc_v = enc[...]
    wg_hi, wg_lo = split(enc_v.astype(F32) * gain[...])

    def put(x, at):
        hi, lo = split(x)
        comp[0 : x.shape[0], at : at + x.shape[1]] = hi
        comp[128 : 128 + x.shape[0], at : at + x.shape[1]] = lo

    put(nt(enc_v, enc_v) * (1.0 / enc_v.shape[1]), 2 * hd)
    for load, w, at in ((loads[6], wk, 0), (loads[7], wv, hd), (loads[8], wq, 2 * hd + 128)):
        load.wait()
        put(nn(wg_hi, w[...]) + nn(wg_lo, w[...]), at)

    def tiled(g):
        pair = jnp.concatenate([g[...]] * 2, axis=1)
        return jnp.concatenate([pair] * (hd // 128), axis=1)

    kg = tiled(k_gain)
    qg = tiled(q_gain) * (math.log2(math.e) / math.sqrt(HEAD_DIM))

    def head_norm(x, eps_u, g):
        sq = (x * x).astype(BF16)
        blk = ones_blk[...]
        mean = jnp.concatenate([nn(sq[:, i : i + 256], blk) for i in range(0, hd, 256)], axis=1)
        return (x * lax.rsqrt(mean + eps_u) * g).astype(BF16)

    def project(f, k_ref, v_ref, at, q_at=None):
        n = f.shape[0]
        two = jnp.concatenate([f, f], axis=1)
        width = 2 * hd + 128 + (hd if q_at is not None else 0)
        y = nn(two, comp[:, 0:width])
        quad = jnp.sum(y[:, 2 * hd : 2 * hd + 128] * f.astype(F32), axis=1, keepdims=True)
        u = jnp.maximum(quad, 0.0) + EPS_ROW
        eps_u = EPS_HEAD * u
        k_ref[pl.ds(at, n), :] = head_norm(y[:, 0:hd], eps_u, kg)
        v_ref[pl.ds(at, n), :] = (y[:, hd : 2 * hd] * lax.rsqrt(u)).astype(BF16)
        if q_at is not None:
            q_s[pl.ds(q_at, n), :] = head_norm(y[:, 2 * hd + 128 :], eps_u, qg)

    crow = chunk_of(rows, 16)
    ccell = crow * cols

    def own_step(i, c):
        f = fext[pl.ds(HALO + i * crow, crow)].reshape(ccell, 128)
        project(f, k_o, v_o, pl.multiple_of(HALO * cols + i * ccell, 16), pl.multiple_of(i * ccell, 16))
        return c

    lax.fori_loop(0, rows // crow, own_step, 0, unroll=8)

    for copy in copies:
        copy.wait_recv()

    for r0 in (0, HALO + rows):
        project(fext[r0 : r0 + HALO].reshape(HALO * cols, 128), k_o, v_o, r0 * cols)

    cpair = chunk_of(pairs + 2 * hp, 14)

    def side_step(i, c):
        for src, k_ref, v_ref in ((halo_l, k_l, v_l), (halo_r, k_r, v_r)):
            f = src[pl.ds(i * cpair, cpair)].reshape(cpair * 16, 128)
            project(f, k_ref, v_ref, pl.multiple_of(i * cpair * 16, 16))
        return c

    lax.fori_loop(0, (pairs + 2 * hp) // cpair, side_step, 0, unroll=5)

    nq = TR * cols
    head = lax.broadcasted_iota(jnp.int32, (nq, 256), 1) // HEAD_DIM

    def attend(t, c):
        slot = jnp.minimum(t, 3) + jnp.maximum(t - (tiles - 4), 0)
        m = masks[slot]
        m4 = jnp.concatenate([m] * 4, axis=0)
        o_at = pl.ds(pl.multiple_of(t * nq, nq), half)
        s_at = pl.ds(pl.multiple_of(t * TR * SIDE, TR * SIDE), side)
        q_at = pl.ds(pl.multiple_of(t * nq, nq), nq)
        for p in range(hd // 256):
            ps = slice(256 * p, 256 * p + 256)
            q = q_s[q_at, ps]
            zero = jnp.zeros_like(q)
            q4 = jnp.concatenate([jnp.where(head == h, q, zero) for h in range(4)], axis=0)
            k = jnp.concatenate([k_o[o_at, ps], k_l[s_at, ps], k_r[s_at, ps]], axis=0)
            v = jnp.concatenate([v_o[o_at, ps], v_l[s_at, ps], v_r[s_at, ps]], axis=0)
            e = jnp.exp2(nt(q4, k)).astype(BF16) * m4
            den = jnp.sum(e.astype(F32), axis=1, keepdims=True)
            acc = nn(e, v) * (1.0 / den)
            out = acc[0:nq]
            for h in range(1, 4):
                out = jnp.where(head == h, acc[h * nq : (h + 1) * nq], out)
            mix[q_at, ps] = out.astype(BF16)
        return c

    lax.fori_loop(0, tiles, attend, 0, unroll=8)

    for copy in copies:
        copy.wait_send()


def out_kernel(fields, w_enc, mix, w_out, out):
    f = fields[...]
    n = f.shape[0] * f.shape[1]
    latents = nn(f.reshape(n, f.shape[2]), w_enc[...]).astype(BF16)
    res = latents.astype(F32) + nn(mix[...], w_out[...])
    out[...] = res.astype(BF16).reshape(out.shape)


def per_device(n_lat, n_lon, fields, row_valid, w_encode, norm_gain, w_query, w_key, w_value, query_gain, key_gain, w_out):
    rows, cols, chan = fields.shape
    d, hd = w_query.shape
    cells = rows * cols
    ext = rows + 2 * HALO
    pairs = ext // 2
    hbm = pl.BlockSpec(memory_space=pltpu.HBM)
    vmem = pl.BlockSpec(memory_space=pltpu.VMEM)
    keys = (TR + 2 * HALO) * (cols + 2 * SIDE)
    mix = pl.pallas_call(
        functools.partial(attend_kernel, n_lat, n_lon, rows, cols, chan, hd),
        out_shape=jax.ShapeDtypeStruct((cells, hd), BF16),
        in_specs=[hbm] * 9,
        out_specs=vmem,
        scratch_shapes=[
            pltpu.VMEM((rows, cols, chan), BF16),
            pltpu.VMEM((ext, cols, 128), BF16),
            pltpu.VMEM((rows // 2, 16, 128), BF16),
            pltpu.VMEM((rows // 2, 16, 128), BF16),
            pltpu.VMEM((pairs, 16, 128), BF16),
            pltpu.VMEM((pairs, 16, 128), BF16),
            pltpu.VMEM((chan, d), BF16),
            pltpu.VMEM((1, d), F32),
            pltpu.VMEM((d, hd), BF16),
            pltpu.VMEM((d, hd), BF16),
            pltpu.VMEM((d, hd), BF16),
            pltpu.VMEM((1, HEAD_DIM), F32),
            pltpu.VMEM((1, HEAD_DIM), F32),
            pltpu.SMEM((rows,), jnp.int32),
            pltpu.VMEM((256, 3 * hd + 128), BF16),
            pltpu.VMEM((256, 256), BF16),
            pltpu.VMEM((cells, hd), BF16),
            pltpu.VMEM((ext * cols, hd), BF16),
            pltpu.VMEM((ext * cols, hd), BF16),
            pltpu.VMEM((ext * SIDE, hd), BF16),
            pltpu.VMEM((ext * SIDE, hd), BF16),
            pltpu.VMEM((ext * SIDE, hd), BF16),
            pltpu.VMEM((ext * SIDE, hd), BF16),
            pltpu.VMEM((7, TR * cols, keys), BF16),
            pltpu.SemaphoreType.DMA((9,)),
            pltpu.SemaphoreType.DMA((8,)),
            pltpu.SemaphoreType.DMA((8,)),
        ],
        compiler_params=pltpu.CompilerParams(
            collective_id=0, has_side_effects=True, vmem_limit_bytes=63 * 1024 * 1024
        ),
    )(
        fields, row_valid, w_encode, norm_gain.reshape(1, d), w_query, w_key, w_value,
        query_gain.reshape(1, HEAD_DIM), key_gain.reshape(1, HEAD_DIM),
    )
    block = chunk_of(rows, 16)
    return pl.pallas_call(
        out_kernel,
        grid=(rows // block,),
        out_shape=jax.ShapeDtypeStruct((rows, cols, d), BF16),
        in_specs=[
            pl.BlockSpec((block, cols, chan), lambda i: (i, 0, 0)),
            pl.BlockSpec((chan, d), lambda i: (0, 0)),
            pl.BlockSpec((block * cols, hd), lambda i: (i, 0)),
            pl.BlockSpec((hd, d), lambda i: (0, 0)),
        ],
        out_specs=pl.BlockSpec((block, cols, d), lambda i: (i, 0, 0)),
        compiler_params=pltpu.CompilerParams(vmem_limit_bytes=63 * 1024 * 1024),
    )(fields, w_encode, mix, w_out)


def solution(mesh):
    return jax.shard_map(
        functools.partial(per_device, mesh.shape["lat"], mesh.shape["lon"]),
        mesh=mesh,
        in_specs=(P("lat", "lon", None), P("lat"), P(), P(), P(), P(), P(), P(), P(), P()),
        out_specs=P("lat", "lon", None),
        check_vma=False,
    )
```

```python
import functools
import math

import jax
import jax.numpy as jnp
from jax import lax
from jax.experimental import pallas as pl
from jax.experimental.pallas import tpu as pltpu
from jax.sharding import PartitionSpec as P

HEADS = 8
HEAD_DIM = 64
HALO = 6
TR = 4
SIDE = 8
EPS_ROW = 1e-05
EPS_HEAD = 1e-06
F32 = jnp.float32
BF16 = jnp.bfloat16
MESH = pl.DeviceIdType.MESH
NT = (((1,), (1,)), ((), ()))


def nn(a, b):
    return jnp.dot(a, b, preferred_element_type=F32)


def nt(a, b):
    return lax.dot_general(a, b, NT, preferred_element_type=F32)


def split(x):
    hi = x.astype(BF16)
    return hi, (x - hi.astype(F32)).astype(BF16)


def chunk_of(count, most):
    return max(c for c in range(1, most + 1) if count % c == 0)


def attend_kernel(
    n_lat, n_lon, rows, cols, chan, hd,
    fields, row_valid, w_enc, norm_gain, w_q, w_k, w_v, query_gain, key_gain,
    mix,
    num_s, den_s, fraw, fext, send_l, send_r, halo_l, halo_r, enc, gain, wq, wk, wv, q_gain, k_gain, valid, comp, ones_blk,
    q_s, k_o, v_o, k_l, v_l, k_r, v_r, masks,
    local_sem, send_sem, recv_sem,
):
    lat, lon = lax.axis_index("lat"), lax.axis_index("lon")
    up, down = lax.rem(lat + n_lat - 1, n_lat), lax.rem(lat + 1, n_lat)
    left, right = lax.rem(lon + n_lon - 1, n_lon), lax.rem(lon + 1, n_lon)
    pairs = rows // 2
    ext = rows + 2 * HALO
    tiles = rows // TR
    hp = HALO // 2

    loads = [
        pltpu.make_async_copy(src, dst, local_sem.at[i])
        for i, (src, dst) in enumerate(
            (
                (fields, fraw), (w_enc, enc), (norm_gain, gain), (row_valid, valid), (query_gain, q_gain),
                (key_gain, k_gain), (w_k, wk), (w_v, wv), (w_q, wq),
            )
        )
    ]
    for load in loads:
        load.start()

    barrier = pltpu.get_barrier_semaphore()
    around = [
        (up, left), (up, lon), (up, right), (lat, left), (lat, right), (down, left), (down, lon), (down, right)
    ]
    for dev in around:
        pl.semaphore_signal(barrier, inc=1, device_id=dev, device_id_type=MESH)

    own = pl.ds(HALO, rows)
    fext[own] = jnp.zeros((rows, cols, 128), BF16)
    send_l[...] = jnp.zeros(send_l.shape, BF16)
    send_r[...] = jnp.zeros(send_r.shape, BF16)
    loads[0].wait()

    def pack(i, c):
        x = fraw[pl.ds(i * 8, 8)]
        fext[pl.ds(HALO + i * 8, 8), :, 0:chan] = x
        x = x.astype(F32)
        send_l[pl.ds(i * 4, 4), :, 0:chan] = x[:, 0:SIDE].reshape(4, 16, chan).astype(BF16)
        send_r[pl.ds(i * 4, 4), :, 0:chan] = x[:, cols - SIDE :].reshape(4, 16, chan).astype(BF16)
        return c

    lax.fori_loop(0, rows // 8, pack, 0)
    pl.semaphore_wait(barrier, 8)

    first, last = pl.ds(0, hp), pl.ds(pairs - hp, hp)
    top, mid, bot = pl.ds(0, hp), pl.ds(hp, pairs), pl.ds(hp + pairs, hp)
    plan = [
        (send_l.at[...], halo_r.at[mid], (lat, left)),
        (send_r.at[...], halo_l.at[mid], (lat, right)),
        (fext.at[pl.ds(HALO, HALO)], fext.at[pl.ds(HALO + rows, HALO)], (up, lon)),
        (fext.at[pl.ds(rows, HALO)], fext.at[pl.ds(0, HALO)], (down, lon)),
        (send_l.at[first], halo_r.at[bot], (up, left)),
        (send_l.at[last], halo_r.at[top], (down, left)),
        (send_r.at[first], halo_l.at[bot], (up, right)),
        (send_r.at[last], halo_l.at[top], (down, right)),
    ]
    copies = [
        pltpu.make_async_remote_copy(
            src_ref=src, dst_ref=dst, send_sem=send_sem.at[i], recv_sem=recv_sem.at[i],
            device_id=dev, device_id_type=MESH,
        )
        for i, (src, dst, dev) in enumerate(plan)
    ]
    for copy in copies:
        copy.start()

    comp[...] = jnp.zeros(comp.shape, BF16)
    row_i = lax.broadcasted_iota(jnp.int32, (256, 256), 0) // HEAD_DIM
    col_i = lax.broadcasted_iota(jnp.int32, (256, 256), 1) // HEAD_DIM
    ones_blk[...] = jnp.where(row_i == col_i, 1.0 / HEAD_DIM, 0.0).astype(BF16)

    keys = (TR + 2 * HALO) * (cols + 2 * SIDE)
    half = (TR + 2 * HALO) * cols
    side = (TR + 2 * HALO) * SIDE
    lane = lax.broadcasted_iota(jnp.int32, (1, keys), 1)
    rel = jnp.where(lane < half, lane, jnp.where(lane < half + side, lane - half, lane - half - side))
    key_row = jnp.where(lane < half, rel // cols, rel // SIDE)
    key_col = jnp.where(
        lane < half, rel % cols, jnp.where(lane < half + side, rel % SIDE - SIDE, rel % SIDE + cols)
    )
    qi = lax.broadcasted_iota(jnp.int32, (TR * cols, 1), 0)
    row_off = key_row - qi // cols
    col_off = key_col - qi % cols
    for load in loads[1:6]:
        load.wait()
    near = (row_off >= 0) & (row_off <= 2 * HALO) & (col_off >= -HALO) & (col_off <= HALO)
    base = jnp.where(near, 1.0, 0.0).astype(F32)
    has_up = jnp.where(lat > 0, 1.0, 0.0).astype(F32)
    has_down = jnp.where(lat < n_lat - 1, 1.0, 0.0).astype(F32)
    for slot, tile in enumerate((0, 1, 2, None, tiles - 3, tiles - 2, tiles - 1)):
        m = base
        if tile is not None:
            ok = jnp.ones((1, keys), F32)
            for r in range(TR + 2 * HALO):
                e = tile * TR + r
                if e < HALO:
                    v = has_up
                elif e >= HALO + rows:
                    v = has_down
                else:
                    v = valid[e - HALO].astype(F32)
                ok = jnp.where(key_row == r, v, ok)
            m = base * ok
        masks[slot] = m.astype(BF16)

    enc_v = enc[...]
    wg_hi, wg_lo = split(enc_v.astype(F32) * gain[...])

    def put(x, at):
        hi, lo = split(x)
        comp[0 : x.shape[0], at : at + x.shape[1]] = hi
        comp[128 : 128 + x.shape[0], at : at + x.shape[1]] = lo

    put(nt(enc_v, enc_v) * (1.0 / enc_v.shape[1]), 2 * hd)
    for load, w, at in ((loads[6], wk, 0), (loads[7], wv, hd), (loads[8], wq, 2 * hd + 128)):
        load.wait()
        put(nn(wg_hi, w[...]) + nn(wg_lo, w[...]), at)

    def tiled(g):
        pair = jnp.concatenate([g[...]] * 2, axis=1)
        return jnp.concatenate([pair] * (hd // 128), axis=1)

    kg = tiled(k_gain)
    qg = tiled(q_gain) * (math.log2(math.e) / math.sqrt(HEAD_DIM))

    def head_norm(x, eps_u, g):
        sq = (x * x).astype(BF16)
        blk = ones_blk[...]
        mean = jnp.concatenate([nn(sq[:, i : i + 256], blk) for i in range(0, hd, 256)], axis=1)
        return (x * lax.rsqrt(mean + eps_u) * g).astype(BF16)

    def project(f, k_ref, v_ref, at, q_at=None):
        n = f.shape[0]
        two = jnp.concatenate([f, f], axis=1)
        width = 2 * hd + 128 + (hd if q_at is not None else 0)
        y = nn(two, comp[:, 0:width])
        quad = jnp.sum(y[:, 2 * hd : 2 * hd + 128] * f.astype(F32), axis=1, keepdims=True)
        u = jnp.maximum(quad, 0.0) + EPS_ROW
        eps_u = EPS_HEAD * u
        k_ref[pl.ds(at, n), :] = head_norm(y[:, 0:hd], eps_u, kg)
        v_ref[pl.ds(at, n), :] = (y[:, hd : 2 * hd] * lax.rsqrt(u)).astype(BF16)
        if q_at is not None:
            q_s[pl.ds(q_at, n), :] = head_norm(y[:, 2 * hd + 128 :], eps_u, qg)

    crow = chunk_of(rows, 16)
    ccell = crow * cols

    def own_step(i, c):
        f = fext[pl.ds(HALO + i * crow, crow)].reshape(ccell, 128)
        project(f, k_o, v_o, pl.multiple_of(HALO * cols + i * ccell, 16), pl.multiple_of(i * ccell, 16))
        return c

    lax.fori_loop(0, rows // crow, own_step, 0, unroll=8)

    nq = TR * cols
    head = lax.broadcasted_iota(jnp.int32, (nq, 256), 1) // HEAD_DIM

    def pick(x):
        y = x[0:nq]
        for h in range(1, 4):
            y = jnp.where(head == h, x[h * nq : (h + 1) * nq], y)
        return y

    def partial(t, p, k, v, lanes):
        ps = slice(256 * p, 256 * p + 256)
        q_at = pl.ds(pl.multiple_of(t * nq, nq), nq)
        slot = jnp.minimum(t, 3) + jnp.maximum(t - (tiles - 4), 0)
        q = q_s[q_at, ps]
        zero = jnp.zeros_like(q)
        q4 = jnp.concatenate([jnp.where(head == h, q, zero) for h in range(4)], axis=0)
        m = masks[slot, :, lanes]
        e = jnp.exp2(nt(q4, k)).astype(BF16) * jnp.concatenate([m] * 4, axis=0)
        den = jnp.sum(e.astype(F32), axis=1, keepdims=True)
        return q_at, ps, pick(nn(e, v)), pick(den)

    def own_part(t, c):
        o_at = pl.ds(pl.multiple_of(t * nq, nq), half)
        for p in range(hd // 256):
            ps = slice(256 * p, 256 * p + 256)
            q_at, ps, num, den = partial(t, p, k_o[o_at, ps], v_o[o_at, ps], slice(0, half))
            num_s[q_at, ps] = num
            den_s[q_at, ps] = den
        return c

    def side_part(t, c):
        s_at = pl.ds(pl.multiple_of(t * TR * SIDE, TR * SIDE), side)
        for p in range(hd // 256):
            ps = slice(256 * p, 256 * p + 256)
            k = jnp.concatenate([k_l[s_at, ps], k_r[s_at, ps]], axis=0)
            v = jnp.concatenate([v_l[s_at, ps], v_r[s_at, ps]], axis=0)
            q_at, ps, num, den = partial(t, p, k, v, slice(half, keys))
            mix[q_at, ps] = ((num_s[q_at, ps] + num) / (den_s[q_at, ps] + den)).astype(BF16)
        return c

    edge = -(-HALO // TR)
    lax.fori_loop(edge, tiles - edge, own_part, 0, unroll=chunk_of(tiles - 2 * edge, 7))

    for copy in copies:
        copy.wait_recv()

    for r0 in (0, HALO + rows):
        project(fext[r0 : r0 + HALO].reshape(HALO * cols, 128), k_o, v_o, r0 * cols)
    for t in (*range(edge), *range(tiles - edge, tiles)):
        own_part(t, 0)

    cpair = chunk_of(pairs + 2 * hp, 14)

    def side_step(i, c):
        for src, k_ref, v_ref in ((halo_l, k_l, v_l), (halo_r, k_r, v_r)):
            f = src[pl.ds(i * cpair, cpair)].reshape(cpair * 16, 128)
            project(f, k_ref, v_ref, pl.multiple_of(i * cpair * 16, 16))
        return c

    lax.fori_loop(0, (pairs + 2 * hp) // cpair, side_step, 0, unroll=5)

    lax.fori_loop(0, tiles, side_part, 0, unroll=8)

    for copy in copies:
        copy.wait_send()


def out_kernel(fields, w_enc, mix, w_out, out):
    f = fields[...]
    n = f.shape[0] * f.shape[1]
    latents = nn(f.reshape(n, f.shape[2]), w_enc[...]).astype(BF16)
    res = latents.astype(F32) + nn(mix[...], w_out[...])
    out[...] = res.astype(BF16).reshape(out.shape)


def per_device(n_lat, n_lon, fields, row_valid, w_encode, norm_gain, w_query, w_key, w_value, query_gain, key_gain, w_out):
    rows, cols, chan = fields.shape
    d, hd = w_query.shape
    cells = rows * cols
    ext = rows + 2 * HALO
    pairs = ext // 2
    hbm = pl.BlockSpec(memory_space=pltpu.HBM)
    vmem = pl.BlockSpec(memory_space=pltpu.VMEM)
    keys = (TR + 2 * HALO) * (cols + 2 * SIDE)
    mix = pl.pallas_call(
        functools.partial(attend_kernel, n_lat, n_lon, rows, cols, chan, hd),
        out_shape=jax.ShapeDtypeStruct((cells, hd), BF16),
        in_specs=[hbm] * 9,
        out_specs=vmem,
        scratch_shapes=[
            pltpu.VMEM((cells, hd), F32),
            pltpu.VMEM((cells, hd), F32),
            pltpu.VMEM((rows, cols, chan), BF16),
            pltpu.VMEM((ext, cols, 128), BF16),
            pltpu.VMEM((rows // 2, 16, 128), BF16),
            pltpu.VMEM((rows // 2, 16, 128), BF16),
            pltpu.VMEM((pairs, 16, 128), BF16),
            pltpu.VMEM((pairs, 16, 128), BF16),
            pltpu.VMEM((chan, d), BF16),
            pltpu.VMEM((1, d), F32),
            pltpu.VMEM((d, hd), BF16),
            pltpu.VMEM((d, hd), BF16),
            pltpu.VMEM((d, hd), BF16),
            pltpu.VMEM((1, HEAD_DIM), F32),
            pltpu.VMEM((1, HEAD_DIM), F32),
            pltpu.SMEM((rows,), jnp.int32),
            pltpu.VMEM((256, 3 * hd + 128), BF16),
            pltpu.VMEM((256, 256), BF16),
            pltpu.VMEM((cells, hd), BF16),
            pltpu.VMEM((ext * cols, hd), BF16),
            pltpu.VMEM((ext * cols, hd), BF16),
            pltpu.VMEM((ext * SIDE, hd), BF16),
            pltpu.VMEM((ext * SIDE, hd), BF16),
            pltpu.VMEM((ext * SIDE, hd), BF16),
            pltpu.VMEM((ext * SIDE, hd), BF16),
            pltpu.VMEM((7, TR * cols, keys), BF16),
            pltpu.SemaphoreType.DMA((9,)),
            pltpu.SemaphoreType.DMA((8,)),
            pltpu.SemaphoreType.DMA((8,)),
        ],
        compiler_params=pltpu.CompilerParams(
            collective_id=0, has_side_effects=True, vmem_limit_bytes=63 * 1024 * 1024
        ),
    )(
        fields, row_valid, w_encode, norm_gain.reshape(1, d), w_query, w_key, w_value,
        query_gain.reshape(1, HEAD_DIM), key_gain.reshape(1, HEAD_DIM),
    )
    block = chunk_of(rows, 32)
    return pl.pallas_call(
        out_kernel,
        grid=(rows // block,),
        out_shape=jax.ShapeDtypeStruct((rows, cols, d), BF16),
        in_specs=[
            pl.BlockSpec((block, cols, chan), lambda i: (i, 0, 0)),
            pl.BlockSpec((chan, d), lambda i: (0, 0)),
            pl.BlockSpec((block * cols, hd), lambda i: (i, 0)),
            pl.BlockSpec((hd, d), lambda i: (0, 0)),
        ],
        out_specs=pl.BlockSpec((block, cols, d), lambda i: (i, 0, 0)),
        compiler_params=pltpu.CompilerParams(vmem_limit_bytes=63 * 1024 * 1024),
    )(fields, w_encode, mix, w_out)


def solution(mesh):
    return jax.shard_map(
        functools.partial(per_device, mesh.shape["lat"], mesh.shape["lon"]),
        mesh=mesh,
        in_specs=(P("lat", "lon", None), P("lat"), P(), P(), P(), P(), P(), P(), P(), P()),
        out_specs=P("lat", "lon", None),
        check_vma=False,
    )
```

```python
import functools
import math

import jax
import jax.numpy as jnp
from jax import lax
from jax.experimental import pallas as pl
from jax.experimental.pallas import tpu as pltpu
from jax.sharding import PartitionSpec as P

HEADS = 8
HEAD_DIM = 64
HALO = 6
TR = 4
SIDE = 8
RING = 8
EPS_ROW = 1e-05
EPS_HEAD = 1e-06
F32 = jnp.float32
BF16 = jnp.bfloat16
MESH = pl.DeviceIdType.MESH
NT = (((1,), (1,)), ((), ()))


def nn(a, b):
    return jnp.dot(a, b, preferred_element_type=F32)


def nt(a, b):
    return lax.dot_general(a, b, NT, preferred_element_type=F32)


def split(x):
    hi = x.astype(BF16)
    return hi, (x - hi.astype(F32)).astype(BF16)


def chunk_of(count, most):
    return max(c for c in range(1, most + 1) if count % c == 0)


def attend_kernel(
    n_lat, n_lon, rows, cols, chan, hd,
    fields, fields_t, row_valid, w_enc, norm_gain, w_q, w_k, w_v, query_gain, key_gain,
    mix,
    num_s, den_s, ft, work, x_l, x_r, c_ul, c_ur, c_dl, c_dr, fraw, fext, send_l, send_r, halo_l, halo_r, enc, gain, wq, wk, wv, q_gain, k_gain, valid, comp, ones_blk,
    q_s, k_o, v_o, k_l, v_l, k_r, v_r, masks,
    local_sem, send_sem, recv_sem,
):
    lat, lon = lax.axis_index("lat"), lax.axis_index("lon")
    up, down = lax.rem(lat + n_lat - 1, n_lat), lax.rem(lat + 1, n_lat)
    left, right = lax.rem(lon + n_lon - 1, n_lon), lax.rem(lon + 1, n_lon)
    ext = rows + 2 * HALO
    tiles = rows // TR

    loads = [
        pltpu.make_async_copy(src, dst, local_sem.at[i])
        for i, (src, dst) in enumerate(
            (
                (fields, fraw), (fields_t, ft), (w_enc, enc), (norm_gain, gain), (row_valid, valid), (query_gain, q_gain),
                (key_gain, k_gain), (w_k, wk), (w_v, wv), (w_q, wq),
            )
        )
    ]
    for load in loads:
        load.start()

    barrier = pltpu.get_barrier_semaphore()
    around = [
        (up, left), (up, lon), (up, right), (lat, left), (lat, right), (down, left), (down, lon), (down, right)
    ]
    for dev in around:
        pl.semaphore_signal(barrier, inc=1, device_id=dev, device_id_type=MESH)

    half_chan = chan // 2
    step = chunk_of(half_chan, 7)
    loads[1].wait()

    def pack(i, c):
        x = ft[pl.ds(i * 2 * step, 2 * step)].astype(F32)
        send_l[pl.ds(i * step, step)] = x[:, 0:SIDE].reshape(step, 16, rows).astype(BF16)
        send_r[pl.ds(i * step, step)] = x[:, cols - SIDE :].reshape(step, 16, rows).astype(BF16)
        return c

    lax.fori_loop(0, half_chan // step, pack, 0)

    head_rows, tail_rows = pl.ds(HALO, HALO), pl.ds(rows, HALO)
    above, below = pl.ds(0, HALO), pl.ds(HALO + rows, HALO)
    plan = [
        (send_l.at[...], halo_r.at[...], (lat, left)),
        (send_r.at[...], halo_l.at[...], (lat, right)),
        (fext.at[head_rows], fext.at[below], (up, lon)),
        (fext.at[tail_rows], fext.at[above], (down, lon)),
        (fext.at[head_rows], c_dr.at[...], (up, left)),
        (fext.at[tail_rows], c_ur.at[...], (down, left)),
        (fext.at[head_rows], c_dl.at[...], (up, right)),
        (fext.at[tail_rows], c_ul.at[...], (down, right)),
    ]
    copies = [
        pltpu.make_async_remote_copy(
            src_ref=src, dst_ref=dst, send_sem=send_sem.at[i], recv_sem=recv_sem.at[i],
            device_id=dev, device_id_type=MESH,
        )
        for i, (src, dst, dev) in enumerate(plan)
    ]

    early = lax.rem(lon, RING) == 0

    def meet():
        pl.semaphore_wait(barrier, 8)
        for copy in copies[:2]:
            copy.start()

    @pl.when(jnp.logical_not(early))
    def _():
        meet()

    fext[pl.ds(HALO, rows)] = jnp.zeros((rows, cols, 128), BF16)
    loads[0].wait()
    fext[pl.ds(HALO, rows), :, 0:chan] = fraw[...]

    @pl.when(jnp.logical_not(early))
    def _():
        for copy in copies[2:]:
            copy.start()

    work[...] = jnp.zeros(work.shape, F32)

    comp[...] = jnp.zeros(comp.shape, BF16)
    row_i = lax.broadcasted_iota(jnp.int32, (256, 256), 0) // HEAD_DIM
    col_i = lax.broadcasted_iota(jnp.int32, (256, 256), 1) // HEAD_DIM
    ones_blk[...] = jnp.where(row_i == col_i, 1.0 / HEAD_DIM, 0.0).astype(BF16)

    keys = (TR + 2 * HALO) * (cols + 2 * SIDE)
    half = (TR + 2 * HALO) * cols
    side = (TR + 2 * HALO) * SIDE
    lane = lax.broadcasted_iota(jnp.int32, (1, keys), 1)
    rel = jnp.where(lane < half, lane, jnp.where(lane < half + side, lane - half, lane - half - side))
    key_row = jnp.where(lane < half, rel // cols, rel // SIDE)
    key_col = jnp.where(
        lane < half, rel % cols, jnp.where(lane < half + side, rel % SIDE - SIDE, rel % SIDE + cols)
    )
    qi = lax.broadcasted_iota(jnp.int32, (TR * cols, 1), 0)
    row_off = key_row - qi // cols
    col_off = key_col - qi % cols
    for load in loads[2:7]:
        load.wait()
    near = (row_off >= 0) & (row_off <= 2 * HALO) & (col_off >= -HALO) & (col_off <= HALO)
    base = jnp.where(near, 1.0, 0.0).astype(F32)
    has_up = jnp.where(lat > 0, 1.0, 0.0).astype(F32)
    has_down = jnp.where(lat < n_lat - 1, 1.0, 0.0).astype(F32)
    for slot, tile in enumerate((0, 1, 2, None, tiles - 3, tiles - 2, tiles - 1)):
        m = base
        if tile is not None:
            ok = jnp.ones((1, keys), F32)
            for r in range(TR + 2 * HALO):
                e = tile * TR + r
                if e < HALO:
                    v = has_up
                elif e >= HALO + rows:
                    v = has_down
                else:
                    v = valid[e - HALO].astype(F32)
                ok = jnp.where(key_row == r, v, ok)
            m = base * ok
        masks[slot] = m.astype(BF16)

    enc_v = enc[...]
    wg_hi, wg_lo = split(enc_v.astype(F32) * gain[...])

    def put(x, at):
        hi, lo = split(x)
        comp[0 : x.shape[0], at : at + x.shape[1]] = hi
        comp[128 : 128 + x.shape[0], at : at + x.shape[1]] = lo

    put(nt(enc_v, enc_v) * (1.0 / enc_v.shape[1]), 2 * hd)
    for load, w, at in ((loads[7], wk, 0), (loads[8], wv, hd), (loads[9], wq, 2 * hd + 128)):
        load.wait()
        put(nn(wg_hi, w[...]) + nn(wg_lo, w[...]), at)

    def tiled(g):
        pair = jnp.concatenate([g[...]] * 2, axis=1)
        return jnp.concatenate([pair] * (hd // 128), axis=1)

    kg = tiled(k_gain)
    qg = tiled(q_gain) * (math.log2(math.e) / math.sqrt(HEAD_DIM))

    def head_norm(x, eps_u, g):
        sq = (x * x).astype(BF16)
        blk = ones_blk[...]
        mean = jnp.concatenate([nn(sq[:, i : i + 256], blk) for i in range(0, hd, 256)], axis=1)
        return (x * lax.rsqrt(mean + eps_u) * g).astype(BF16)

    def project(f, k_ref, v_ref, at, q_at=None):
        n = f.shape[0]
        two = jnp.concatenate([f, f], axis=1)
        width = 2 * hd + 128 + (hd if q_at is not None else 0)
        y = nn(two, comp[:, 0:width])
        quad = jnp.sum(y[:, 2 * hd : 2 * hd + 128] * f.astype(F32), axis=1, keepdims=True)
        u = jnp.maximum(quad, 0.0) + EPS_ROW
        eps_u = EPS_HEAD * u
        k_ref[pl.ds(at, n), :] = head_norm(y[:, 0:hd], eps_u, kg)
        v_ref[pl.ds(at, n), :] = (y[:, hd : 2 * hd] * lax.rsqrt(u)).astype(BF16)
        if q_at is not None:
            q_s[pl.ds(q_at, n), :] = head_norm(y[:, 2 * hd + 128 :], eps_u, qg)

    crow = chunk_of(rows, 16)
    ccell = crow * cols

    def own_step(i, c):
        f = fext[pl.ds(HALO + i * crow, crow)].reshape(ccell, 128)
        project(f, k_o, v_o, pl.multiple_of(HALO * cols + i * ccell, 16), pl.multiple_of(i * ccell, 16))
        return c

    lax.fori_loop(0, rows // crow, own_step, 0, unroll=8)

    @pl.when(early)
    def _():
        meet()
        for copy in copies[2:]:
            copy.start()

    nq = TR * cols
    head = lax.broadcasted_iota(jnp.int32, (nq, 256), 1) // HEAD_DIM

    def pick(x):
        y = x[0:nq]
        for h in range(1, 4):
            y = jnp.where(head == h, x[h * nq : (h + 1) * nq], y)
        return y

    def partial(t, p, k, v, lanes):
        ps = slice(256 * p, 256 * p + 256)
        q_at = pl.ds(pl.multiple_of(t * nq, nq), nq)
        slot = jnp.minimum(t, 3) + jnp.maximum(t - (tiles - 4), 0)
        q = q_s[q_at, ps]
        zero = jnp.zeros_like(q)
        q4 = jnp.concatenate([jnp.where(head == h, q, zero) for h in range(4)], axis=0)
        m = masks[slot, :, lanes]
        e = jnp.exp2(nt(q4, k)).astype(BF16) * jnp.concatenate([m] * 4, axis=0)
        den = jnp.sum(e.astype(F32), axis=1, keepdims=True)
        return q_at, ps, pick(nn(e, v)), pick(den)

    def own_part(t, c):
        o_at = pl.ds(pl.multiple_of(t * nq, nq), half)
        for p in range(hd // 256):
            ps = slice(256 * p, 256 * p + 256)
            q_at, ps, num, den = partial(t, p, k_o[o_at, ps], v_o[o_at, ps], slice(0, half))
            num_s[q_at, ps] = num
            den_s[q_at, ps] = den
        return c

    def side_part(t, c):
        s_at = pl.ds(pl.multiple_of(t * TR * SIDE, TR * SIDE), side)
        for p in range(hd // 256):
            ps = slice(256 * p, 256 * p + 256)
            k = jnp.concatenate([k_l[s_at, ps], k_r[s_at, ps]], axis=0)
            v = jnp.concatenate([v_l[s_at, ps], v_r[s_at, ps]], axis=0)
            q_at, ps, num, den = partial(t, p, k, v, slice(half, keys))
            mix[q_at, ps] = ((num_s[q_at, ps] + num) / (den_s[q_at, ps] + den)).astype(BF16)
        return c

    edge = -(-HALO // TR)
    lax.fori_loop(edge, tiles - edge, own_part, 0, unroll=chunk_of(tiles - 2 * edge, 7))

    for copy in copies:
        copy.wait_recv()

    for r0 in (0, HALO + rows):
        project(fext[r0 : r0 + HALO].reshape(HALO * cols, 128), k_o, v_o, r0 * cols)
    for t in (*range(edge), *range(tiles - edge, tiles)):
        own_part(t, 0)

    lead = HALO * SIDE
    for halo, x_ref, up_ref, down_ref, at in (
        (halo_l, x_l, c_ul, c_dl, cols - SIDE), (halo_r, x_r, c_ur, c_dr, 0)
    ):
        work[0 : chan * SIDE, :] = halo[...].astype(F32).reshape(chan * SIDE, rows)
        x_ref[0:lead, :] = up_ref[...].astype(F32)[:, at : at + SIDE].reshape(lead, 128)
        x_ref[lead + rows * SIDE :, :] = down_ref[...].astype(F32)[:, at : at + SIDE].reshape(lead, 128)
        for c in range(SIDE):
            block = work[pl.ds(c, 128, stride=SIDE), :]
            x_ref[pl.ds(lead + c, rows, stride=SIDE), :] = block.T

    cside = chunk_of(ext // 2, 14) * 2 * SIDE

    def side_step(i, c):
        for x_ref, k_ref, v_ref in ((x_l, k_l, v_l), (x_r, k_r, v_r)):
            at = pl.multiple_of(i * cside, 16)
            project(x_ref[pl.ds(at, cside), :].astype(BF16), k_ref, v_ref, at)
        return c

    lax.fori_loop(0, ext * SIDE // cside, side_step, 0, unroll=5)

    lax.fori_loop(0, tiles, side_part, 0, unroll=8)

    for copy in copies:
        copy.wait_send()


def out_kernel(fields, w_enc, mix, w_out, out):
    f = fields[...]
    n = f.shape[0] * f.shape[1]
    latents = nn(f.reshape(n, f.shape[2]), w_enc[...]).astype(BF16)
    res = latents.astype(F32) + nn(mix[...], w_out[...])
    out[...] = res.astype(BF16).reshape(out.shape)


def per_device(n_lat, n_lon, fields, row_valid, w_encode, norm_gain, w_query, w_key, w_value, query_gain, key_gain, w_out):
    rows, cols, chan = fields.shape
    d, hd = w_query.shape
    cells = rows * cols
    ext = rows + 2 * HALO
    fields_t = jnp.transpose(fields, (2, 1, 0))
    hbm = pl.BlockSpec(memory_space=pltpu.HBM)
    vmem = pl.BlockSpec(memory_space=pltpu.VMEM)
    keys = (TR + 2 * HALO) * (cols + 2 * SIDE)
    mix = pl.pallas_call(
        functools.partial(attend_kernel, n_lat, n_lon, rows, cols, chan, hd),
        out_shape=jax.ShapeDtypeStruct((cells, hd), BF16),
        in_specs=[hbm] * 10,
        out_specs=vmem,
        scratch_shapes=[
            pltpu.VMEM((cells, hd), F32),
            pltpu.VMEM((cells, hd), F32),
            pltpu.VMEM((chan, cols, rows), BF16),
            pltpu.VMEM((128 * SIDE, rows), F32),
            pltpu.VMEM((ext * SIDE, 128), F32),
            pltpu.VMEM((ext * SIDE, 128), F32),
            pltpu.VMEM((HALO, cols, 128), BF16),
            pltpu.VMEM((HALO, cols, 128), BF16),
            pltpu.VMEM((HALO, cols, 128), BF16),
            pltpu.VMEM((HALO, cols, 128), BF16),
            pltpu.VMEM((rows, cols, chan), BF16),
            pltpu.VMEM((ext, cols, 128), BF16),
            pltpu.VMEM((chan // 2, 16, rows), BF16),
            pltpu.VMEM((chan // 2, 16, rows), BF16),
            pltpu.VMEM((chan // 2, 16, rows), BF16),
            pltpu.VMEM((chan // 2, 16, rows), BF16),
            pltpu.VMEM((chan, d), BF16),
            pltpu.VMEM((1, d), F32),
            pltpu.VMEM((d, hd), BF16),
            pltpu.VMEM((d, hd), BF16),
            pltpu.VMEM((d, hd), BF16),
            pltpu.VMEM((1, HEAD_DIM), F32),
            pltpu.VMEM((1, HEAD_DIM), F32),
            pltpu.SMEM((rows,), jnp.int32),
            pltpu.VMEM((256, 3 * hd + 128), BF16),
            pltpu.VMEM((256, 256), BF16),
            pltpu.VMEM((cells, hd), BF16),
            pltpu.VMEM((ext * cols, hd), BF16),
            pltpu.VMEM((ext * cols, hd), BF16),
            pltpu.VMEM((ext * SIDE, hd), BF16),
            pltpu.VMEM((ext * SIDE, hd), BF16),
            pltpu.VMEM((ext * SIDE, hd), BF16),
            pltpu.VMEM((ext * SIDE, hd), BF16),
            pltpu.VMEM((7, TR * cols, keys), BF16),
            pltpu.SemaphoreType.DMA((10,)),
            pltpu.SemaphoreType.DMA((8,)),
            pltpu.SemaphoreType.DMA((8,)),
        ],
        compiler_params=pltpu.CompilerParams(
            collective_id=0, has_side_effects=True, vmem_limit_bytes=63 * 1024 * 1024
        ),
    )(
        fields, fields_t, row_valid, w_encode, norm_gain.reshape(1, d), w_query, w_key, w_value,
        query_gain.reshape(1, HEAD_DIM), key_gain.reshape(1, HEAD_DIM),
    )
    block = chunk_of(rows, 32)
    return pl.pallas_call(
        out_kernel,
        grid=(rows // block,),
        out_shape=jax.ShapeDtypeStruct((rows, cols, d), BF16),
        in_specs=[
            pl.BlockSpec((block, cols, chan), lambda i: (i, 0, 0)),
            pl.BlockSpec((chan, d), lambda i: (0, 0)),
            pl.BlockSpec((block * cols, hd), lambda i: (i, 0)),
            pl.BlockSpec((hd, d), lambda i: (0, 0)),
        ],
        out_specs=pl.BlockSpec((block, cols, d), lambda i: (i, 0, 0)),
        compiler_params=pltpu.CompilerParams(vmem_limit_bytes=63 * 1024 * 1024),
    )(fields, w_encode, mix, w_out)


def solution(mesh):
    return jax.shard_map(
        functools.partial(per_device, mesh.shape["lat"], mesh.shape["lon"]),
        mesh=mesh,
        in_specs=(P("lat", "lon", None), P("lat"), P(), P(), P(), P(), P(), P(), P(), P()),
        out_specs=P("lat", "lon", None),
        check_vma=False,
    )
```

```python
import functools
import math

import jax
import jax.numpy as jnp
from jax import lax
from jax.experimental import pallas as pl
from jax.experimental.pallas import tpu as pltpu
from jax.sharding import PartitionSpec as P

HEADS = 8
HEAD_DIM = 64
HALO = 6
TR = 4
SIDE = 8
RING = 8
EPS_ROW = 1e-05
EPS_HEAD = 1e-06
F32 = jnp.float32
BF16 = jnp.bfloat16
MESH = pl.DeviceIdType.MESH
NT = (((1,), (1,)), ((), ()))


def nn(a, b):
    return jnp.dot(a, b, preferred_element_type=F32)


def nt(a, b):
    return lax.dot_general(a, b, NT, preferred_element_type=F32)


def split(x):
    hi = x.astype(BF16)
    return hi, (x - hi.astype(F32)).astype(BF16)


def chunk_of(count, most):
    return max(c for c in range(1, most + 1) if count % c == 0)


def attend_kernel(
    n_lat, n_lon, rows, cols, chan, hd,
    fields_t, row_valid, w_enc, norm_gain, w_q, w_k, w_v, query_gain, key_gain,
    mix, cells_out,
    num_s, den_s, ft, work, cell_f, x_l, x_r, c_ul, c_ur, c_dl, c_dr, fext, send_l, send_r, halo_l, halo_r, enc, gain, wq, wk, wv, q_gain, k_gain, valid, comp, ones_blk,
    q_s, k_o, v_o, k_l, v_l, k_r, v_r, masks,
    local_sem, send_sem, recv_sem, out_sem,
):
    lat, lon = lax.axis_index("lat"), lax.axis_index("lon")
    up, down = lax.rem(lat + n_lat - 1, n_lat), lax.rem(lat + 1, n_lat)
    left, right = lax.rem(lon + n_lon - 1, n_lon), lax.rem(lon + 1, n_lon)
    ext = rows + 2 * HALO
    tiles = rows // TR

    loads = [
        pltpu.make_async_copy(src, dst, local_sem.at[i])
        for i, (src, dst) in enumerate(
            (
                (fields_t, ft), (w_enc, enc), (norm_gain, gain), (row_valid, valid), (query_gain, q_gain),
                (key_gain, k_gain), (w_k, wk), (w_v, wv), (w_q, wq),
            )
        )
    ]
    for load in loads:
        load.start()

    barrier = pltpu.get_barrier_semaphore()
    around = [
        (up, left), (up, lon), (up, right), (lat, left), (lat, right), (down, left), (down, lon), (down, right)
    ]
    for dev in around:
        pl.semaphore_signal(barrier, inc=1, device_id=dev, device_id_type=MESH)

    work[chan * cols :, :] = jnp.zeros((work.shape[0] - chan * cols, rows), F32)
    x_l[...] = jnp.zeros(x_l.shape, F32)
    x_r[...] = jnp.zeros(x_r.shape, F32)
    loads[0].wait()
    work[0 : chan * cols, :] = ft[...].astype(F32).reshape(chan * cols, rows)
    deep = send_l.shape[1]
    for c in range(HALO):
        send_l[c] = work[pl.ds(c, deep, stride=cols), :].astype(BF16)
        send_r[c] = work[pl.ds(cols - HALO + c, deep, stride=cols), :].astype(BF16)

    head_rows, tail_rows = pl.ds(HALO, HALO), pl.ds(rows, HALO)
    above, below = pl.ds(0, HALO), pl.ds(HALO + rows, HALO)
    plan = [
        (send_l.at[...], halo_r.at[...], (lat, left)),
        (send_r.at[...], halo_l.at[...], (lat, right)),
        (fext.at[head_rows], fext.at[below], (up, lon)),
        (fext.at[tail_rows], fext.at[above], (down, lon)),
        (fext.at[head_rows], c_dr.at[...], (up, left)),
        (fext.at[tail_rows], c_ur.at[...], (down, left)),
        (fext.at[head_rows], c_dl.at[...], (up, right)),
        (fext.at[tail_rows], c_ul.at[...], (down, right)),
    ]
    copies = [
        pltpu.make_async_remote_copy(
            src_ref=src, dst_ref=dst, send_sem=send_sem.at[i], recv_sem=recv_sem.at[i],
            device_id=dev, device_id_type=MESH,
        )
        for i, (src, dst, dev) in enumerate(plan)
    ]

    early = lax.rem(lon, RING) == 0

    def meet():
        pl.semaphore_wait(barrier, 8)
        for copy in copies[:2]:
            copy.start()

    @pl.when(jnp.logical_not(early))
    def _():
        meet()

    for c in range(cols):
        cell_f[pl.ds(c, rows, stride=cols), :] = work[pl.ds(c, 128, stride=cols), :].T
    fext[pl.ds(HALO, rows)] = cell_f[...].astype(BF16).reshape(rows, cols, 128)
    to_hbm = pltpu.make_async_copy(fext.at[pl.ds(HALO, rows)], cells_out, out_sem)
    to_hbm.start()

    @pl.when(jnp.logical_not(early))
    def _():
        for copy in copies[2:]:
            copy.start()

    comp[...] = jnp.zeros(comp.shape, BF16)
    row_i = lax.broadcasted_iota(jnp.int32, (256, 256), 0) // HEAD_DIM
    col_i = lax.broadcasted_iota(jnp.int32, (256, 256), 1) // HEAD_DIM
    ones_blk[...] = jnp.where(row_i == col_i, 1.0 / HEAD_DIM, 0.0).astype(BF16)

    keys = (TR + 2 * HALO) * (cols + 2 * SIDE)
    half = (TR + 2 * HALO) * cols
    side = (TR + 2 * HALO) * SIDE
    lane = lax.broadcasted_iota(jnp.int32, (1, keys), 1)
    rel = jnp.where(lane < half, lane, jnp.where(lane < half + side, lane - half, lane - half - side))
    key_row = jnp.where(lane < half, rel // cols, rel // SIDE)
    key_col = jnp.where(
        lane < half, rel % cols, jnp.where(lane < half + side, rel % SIDE - SIDE, rel % SIDE + cols)
    )
    qi = lax.broadcasted_iota(jnp.int32, (TR * cols, 1), 0)
    row_off = key_row - qi // cols
    col_off = key_col - qi % cols
    for load in loads[1:6]:
        load.wait()
    near = (row_off >= 0) & (row_off <= 2 * HALO) & (col_off >= -HALO) & (col_off <= HALO)
    base = jnp.where(near, 1.0, 0.0).astype(F32)
    has_up = jnp.where(lat > 0, 1.0, 0.0).astype(F32)
    has_down = jnp.where(lat < n_lat - 1, 1.0, 0.0).astype(F32)
    for slot, tile in enumerate((0, 1, 2, None, tiles - 3, tiles - 2, tiles - 1)):
        m = base
        if tile is not None:
            ok = jnp.ones((1, keys), F32)
            for r in range(TR + 2 * HALO):
                e = tile * TR + r
                if e < HALO:
                    v = has_up
                elif e >= HALO + rows:
                    v = has_down
                else:
                    v = valid[e - HALO].astype(F32)
                ok = jnp.where(key_row == r, v, ok)
            m = base * ok
        masks[slot] = m.astype(BF16)

    enc_v = enc[...]
    wg_hi, wg_lo = split(enc_v.astype(F32) * gain[...])

    def put(x, at):
        hi, lo = split(x)
        comp[0 : x.shape[0], at : at + x.shape[1]] = hi
        comp[128 : 128 + x.shape[0], at : at + x.shape[1]] = lo

    put(nt(enc_v, enc_v) * (1.0 / enc_v.shape[1]), 2 * hd)
    for load, w, at in ((loads[6], wk, 0), (loads[7], wv, hd), (loads[8], wq, 2 * hd + 128)):
        load.wait()
        put(nn(wg_hi, w[...]) + nn(wg_lo, w[...]), at)

    def tiled(g):
        pair = jnp.concatenate([g[...]] * 2, axis=1)
        return jnp.concatenate([pair] * (hd // 128), axis=1)

    kg = tiled(k_gain)
    qg = tiled(q_gain) * (math.log2(math.e) / math.sqrt(HEAD_DIM))

    def head_norm(x, eps_u, g):
        sq = (x * x).astype(BF16)
        blk = ones_blk[...]
        mean = jnp.concatenate([nn(sq[:, i : i + 256], blk) for i in range(0, hd, 256)], axis=1)
        return (x * lax.rsqrt(mean + eps_u) * g).astype(BF16)

    def project(f, k_ref, v_ref, at, q_at=None):
        n = f.shape[0]
        two = jnp.concatenate([f, f], axis=1)
        width = 2 * hd + 128 + (hd if q_at is not None else 0)
        y = nn(two, comp[:, 0:width])
        quad = jnp.sum(y[:, 2 * hd : 2 * hd + 128] * f.astype(F32), axis=1, keepdims=True)
        u = jnp.maximum(quad, 0.0) + EPS_ROW
        eps_u = EPS_HEAD * u
        k_ref[pl.ds(at, n), :] = head_norm(y[:, 0:hd], eps_u, kg)
        v_ref[pl.ds(at, n), :] = (y[:, hd : 2 * hd] * lax.rsqrt(u)).astype(BF16)
        if q_at is not None:
            q_s[pl.ds(q_at, n), :] = head_norm(y[:, 2 * hd + 128 :], eps_u, qg)

    crow = chunk_of(rows, 16)
    ccell = crow * cols

    def own_step(i, c):
        f = fext[pl.ds(HALO + i * crow, crow)].reshape(ccell, 128)
        project(f, k_o, v_o, pl.multiple_of(HALO * cols + i * ccell, 16), pl.multiple_of(i * ccell, 16))
        return c

    lax.fori_loop(0, rows // crow, own_step, 0, unroll=8)

    @pl.when(early)
    def _():
        meet()
        for copy in copies[2:]:
            copy.start()

    nq = TR * cols
    head = lax.broadcasted_iota(jnp.int32, (nq, 256), 1) // HEAD_DIM

    def pick(x):
        y = x[0:nq]
        for h in range(1, 4):
            y = jnp.where(head == h, x[h * nq : (h + 1) * nq], y)
        return y

    def partial(t, p, k, v, lanes):
        ps = slice(256 * p, 256 * p + 256)
        q_at = pl.ds(pl.multiple_of(t * nq, nq), nq)
        slot = jnp.minimum(t, 3) + jnp.maximum(t - (tiles - 4), 0)
        q = q_s[q_at, ps]
        zero = jnp.zeros_like(q)
        q4 = jnp.concatenate([jnp.where(head == h, q, zero) for h in range(4)], axis=0)
        m = masks[slot, :, lanes]
        e = jnp.exp2(nt(q4, k)).astype(BF16) * jnp.concatenate([m] * 4, axis=0)
        den = jnp.sum(e.astype(F32), axis=1, keepdims=True)
        return q_at, ps, pick(nn(e, v)), pick(den)

    def own_part(t, c):
        o_at = pl.ds(pl.multiple_of(t * nq, nq), half)
        for p in range(hd // 256):
            ps = slice(256 * p, 256 * p + 256)
            q_at, ps, num, den = partial(t, p, k_o[o_at, ps], v_o[o_at, ps], slice(0, half))
            num_s[q_at, ps] = num
            den_s[q_at, ps] = den
        return c

    def side_part(t, c):
        s_at = pl.ds(pl.multiple_of(t * TR * SIDE, TR * SIDE), side)
        for p in range(hd // 256):
            ps = slice(256 * p, 256 * p + 256)
            k = jnp.concatenate([k_l[s_at, ps], k_r[s_at, ps]], axis=0)
            v = jnp.concatenate([v_l[s_at, ps], v_r[s_at, ps]], axis=0)
            q_at, ps, num, den = partial(t, p, k, v, slice(half, keys))
            mix[q_at, ps] = ((num_s[q_at, ps] + num) / (den_s[q_at, ps] + den)).astype(BF16)
        return c

    edge = -(-HALO // TR)
    lax.fori_loop(edge, tiles - edge, own_part, 0, unroll=chunk_of(tiles - 2 * edge, 7))

    for copy in copies:
        copy.wait_recv()

    for r0 in (0, HALO + rows):
        project(fext[r0 : r0 + HALO].reshape(HALO * cols, 128), k_o, v_o, r0 * cols)
    for t in (*range(edge), *range(tiles - edge, tiles)):
        own_part(t, 0)

    lead = HALO * SIDE
    pad = jnp.zeros((128 - deep, rows), F32)
    for halo, x_ref, up_ref, down_ref, at, slot in (
        (halo_l, x_l, c_ul, c_dl, cols - SIDE, SIDE - HALO), (halo_r, x_r, c_ur, c_dr, 0, 0)
    ):
        x_ref[0:lead, :] = up_ref[...].astype(F32)[:, at : at + SIDE].reshape(lead, 128)
        x_ref[lead + rows * SIDE :, :] = down_ref[...].astype(F32)[:, at : at + SIDE].reshape(lead, 128)
        for c in range(HALO):
            block = jnp.concatenate([halo[c].astype(F32), pad], axis=0)
            x_ref[pl.ds(lead + slot + c, rows, stride=SIDE), :] = block.T

    cside = chunk_of(ext // 2, 14) * 2 * SIDE

    def side_step(i, c):
        for x_ref, k_ref, v_ref in ((x_l, k_l, v_l), (x_r, k_r, v_r)):
            at = pl.multiple_of(i * cside, 16)
            project(x_ref[pl.ds(at, cside), :].astype(BF16), k_ref, v_ref, at)
        return c

    lax.fori_loop(0, ext * SIDE // cside, side_step, 0, unroll=5)

    lax.fori_loop(0, tiles, side_part, 0, unroll=8)

    for copy in copies:
        copy.wait_send()
    to_hbm.wait()


def out_kernel(fields, w_enc, mix, w_out, out):
    f = fields[...]
    n = f.shape[0] * f.shape[1]
    latents = nn(f.reshape(n, f.shape[2])[:, 0 : w_enc.shape[0]], w_enc[...]).astype(BF16)
    res = latents.astype(F32) + nn(mix[...], w_out[...])
    out[...] = res.astype(BF16).reshape(out.shape)


def per_device(n_lat, n_lon, fields, row_valid, w_encode, norm_gain, w_query, w_key, w_value, query_gain, key_gain, w_out):
    rows, cols, chan = fields.shape
    d, hd = w_query.shape
    cells = rows * cols
    ext = rows + 2 * HALO
    fields_t = jnp.transpose(fields, (2, 1, 0))
    deep = -(-chan // 16) * 16
    hbm = pl.BlockSpec(memory_space=pltpu.HBM)
    vmem = pl.BlockSpec(memory_space=pltpu.VMEM)
    keys = (TR + 2 * HALO) * (cols + 2 * SIDE)
    mix, by_cell = pl.pallas_call(
        functools.partial(attend_kernel, n_lat, n_lon, rows, cols, chan, hd),
        out_shape=(jax.ShapeDtypeStruct((cells, hd), BF16), jax.ShapeDtypeStruct((rows, cols, 128), BF16)),
        in_specs=[hbm] * 9,
        out_specs=(vmem, hbm),
        scratch_shapes=[
            pltpu.VMEM((cells, hd), F32),
            pltpu.VMEM((cells, hd), F32),
            pltpu.VMEM((chan, cols, rows), BF16),
            pltpu.VMEM((128 * cols, rows), F32),
            pltpu.VMEM((cells, 128), F32),
            pltpu.VMEM((ext * SIDE, 128), F32),
            pltpu.VMEM((ext * SIDE, 128), F32),
            pltpu.VMEM((HALO, cols, 128), BF16),
            pltpu.VMEM((HALO, cols, 128), BF16),
            pltpu.VMEM((HALO, cols, 128), BF16),
            pltpu.VMEM((HALO, cols, 128), BF16),
            pltpu.VMEM((ext, cols, 128), BF16),
            pltpu.VMEM((HALO, deep, rows), BF16),
            pltpu.VMEM((HALO, deep, rows), BF16),
            pltpu.VMEM((HALO, deep, rows), BF16),
            pltpu.VMEM((HALO, deep, rows), BF16),
            pltpu.VMEM((chan, d), BF16),
            pltpu.VMEM((1, d), F32),
            pltpu.VMEM((d, hd), BF16),
            pltpu.VMEM((d, hd), BF16),
            pltpu.VMEM((d, hd), BF16),
            pltpu.VMEM((1, HEAD_DIM), F32),
            pltpu.VMEM((1, HEAD_DIM), F32),
            pltpu.SMEM((rows,), jnp.int32),
            pltpu.VMEM((256, 3 * hd + 128), BF16),
            pltpu.VMEM((256, 256), BF16),
            pltpu.VMEM((cells, hd), BF16),
            pltpu.VMEM((ext * cols, hd), BF16),
            pltpu.VMEM((ext * cols, hd), BF16),
            pltpu.VMEM((ext * SIDE, hd), BF16),
            pltpu.VMEM((ext * SIDE, hd), BF16),
            pltpu.VMEM((ext * SIDE, hd), BF16),
            pltpu.VMEM((ext * SIDE, hd), BF16),
            pltpu.VMEM((7, TR * cols, keys), BF16),
            pltpu.SemaphoreType.DMA((9,)),
            pltpu.SemaphoreType.DMA((8,)),
            pltpu.SemaphoreType.DMA((8,)),
            pltpu.SemaphoreType.DMA,
        ],
        compiler_params=pltpu.CompilerParams(
            collective_id=0, has_side_effects=True, vmem_limit_bytes=63 * 1024 * 1024
        ),
    )(
        fields_t, row_valid, w_encode, norm_gain.reshape(1, d), w_query, w_key, w_value,
        query_gain.reshape(1, HEAD_DIM), key_gain.reshape(1, HEAD_DIM),
    )
    block = chunk_of(rows, 32)
    return pl.pallas_call(
        out_kernel,
        grid=(rows // block,),
        out_shape=jax.ShapeDtypeStruct((rows, cols, d), BF16),
        in_specs=[
            pl.BlockSpec((block, cols, 128), lambda i: (i, 0, 0)),
            pl.BlockSpec((chan, d), lambda i: (0, 0)),
            pl.BlockSpec((block * cols, hd), lambda i: (i, 0)),
            pl.BlockSpec((hd, d), lambda i: (0, 0)),
        ],
        out_specs=pl.BlockSpec((block, cols, d), lambda i: (i, 0, 0)),
        compiler_params=pltpu.CompilerParams(vmem_limit_bytes=63 * 1024 * 1024),
    )(by_cell, w_encode, mix, w_out)


def solution(mesh):
    return jax.shard_map(
        functools.partial(per_device, mesh.shape["lat"], mesh.shape["lon"]),
        mesh=mesh,
        in_specs=(P("lat", "lon", None), P("lat"), P(), P(), P(), P(), P(), P(), P(), P()),
        out_specs=P("lat", "lon", None),
        check_vma=False,
    )
```

```python
import functools
import math

import jax
import jax.numpy as jnp
from jax import lax
from jax.experimental import pallas as pl
from jax.experimental.pallas import tpu as pltpu
from jax.sharding import PartitionSpec as P

HEADS = 8
HEAD_DIM = 64
HALO = 6
TR = 4
SR = 16
SIDE = 8
SUNROLL = 8
RING = 8
EPS_ROW = 1e-05
EPS_HEAD = 1e-06
F32 = jnp.float32
BF16 = jnp.bfloat16
MESH = pl.DeviceIdType.MESH
NT = (((1,), (1,)), ((), ()))


def nn(a, b):
    return jnp.dot(a, b, preferred_element_type=F32)


def nt(a, b):
    return lax.dot_general(a, b, NT, preferred_element_type=F32)


def split(x):
    hi = x.astype(BF16)
    return hi, (x - hi.astype(F32)).astype(BF16)


def chunk_of(count, most):
    return max(c for c in range(1, most + 1) if count % c == 0)


def attend_kernel(
    n_lat, n_lon, rows, cols, chan, hd,
    fields_t, row_valid, w_enc, norm_gain, w_q, w_k, w_v, query_gain, key_gain,
    mix, cells_out,
    num_l, num_r, den_l, den_r, q_l, q_r, smasks, ft, work, cell_f, x_l, x_r, c_ul, c_ur, c_dl, c_dr, fext, send_l, send_r, halo_l, halo_r, enc, gain, wq, wk, wv, q_gain, k_gain, valid, comp, ones_blk,
    q_s, k_o, v_o, k_l, v_l, k_r, v_r, masks,
    local_sem, send_sem, recv_sem, out_sem,
):
    lat, lon = lax.axis_index("lat"), lax.axis_index("lon")
    up, down = lax.rem(lat + n_lat - 1, n_lat), lax.rem(lat + 1, n_lat)
    left, right = lax.rem(lon + n_lon - 1, n_lon), lax.rem(lon + 1, n_lon)
    ext = rows + 2 * HALO
    tiles = rows // TR

    loads = [
        pltpu.make_async_copy(src, dst, local_sem.at[i])
        for i, (src, dst) in enumerate(
            (
                (fields_t, ft), (w_enc, enc), (norm_gain, gain), (row_valid, valid), (query_gain, q_gain),
                (key_gain, k_gain), (w_k, wk), (w_v, wv), (w_q, wq),
            )
        )
    ]
    for load in loads:
        load.start()

    barrier = pltpu.get_barrier_semaphore()
    around = [
        (up, left), (up, lon), (up, right), (lat, left), (lat, right), (down, left), (down, lon), (down, right)
    ]
    for dev in around:
        pl.semaphore_signal(barrier, inc=1, device_id=dev, device_id_type=MESH)

    work[chan * cols :, :] = jnp.zeros((work.shape[0] - chan * cols, rows), F32)
    x_l[...] = jnp.zeros(x_l.shape, F32)
    x_r[...] = jnp.zeros(x_r.shape, F32)
    loads[0].wait()
    work[0 : chan * cols, :] = ft[...].astype(F32).reshape(chan * cols, rows)
    deep = send_l.shape[1]
    for c in range(HALO):
        send_l[c] = work[pl.ds(c, deep, stride=cols), :].astype(BF16)
        send_r[c] = work[pl.ds(cols - HALO + c, deep, stride=cols), :].astype(BF16)

    head_rows, tail_rows = pl.ds(HALO, HALO), pl.ds(rows, HALO)
    above, below = pl.ds(0, HALO), pl.ds(HALO + rows, HALO)
    plan = [
        (send_l.at[...], halo_r.at[...], (lat, left)),
        (send_r.at[...], halo_l.at[...], (lat, right)),
        (fext.at[head_rows], fext.at[below], (up, lon)),
        (fext.at[tail_rows], fext.at[above], (down, lon)),
        (fext.at[head_rows], c_dr.at[...], (up, left)),
        (fext.at[tail_rows], c_ur.at[...], (down, left)),
        (fext.at[head_rows], c_dl.at[...], (up, right)),
        (fext.at[tail_rows], c_ul.at[...], (down, right)),
    ]
    copies = [
        pltpu.make_async_remote_copy(
            src_ref=src, dst_ref=dst, send_sem=send_sem.at[i], recv_sem=recv_sem.at[i],
            device_id=dev, device_id_type=MESH,
        )
        for i, (src, dst, dev) in enumerate(plan)
    ]

    early = lax.rem(lon, RING) == 0

    def meet():
        pl.semaphore_wait(barrier, 8)
        for copy in copies[:2]:
            copy.start()

    @pl.when(jnp.logical_not(early))
    def _():
        meet()

    for c in range(cols):
        cell_f[pl.ds(c, rows, stride=cols), :] = work[pl.ds(c, 128, stride=cols), :].T
    fext[pl.ds(HALO, rows)] = cell_f[...].astype(BF16).reshape(rows, cols, 128)
    to_hbm = pltpu.make_async_copy(fext.at[pl.ds(HALO, rows)], cells_out, out_sem)
    to_hbm.start()

    @pl.when(jnp.logical_not(early))
    def _():
        for copy in copies[2:]:
            copy.start()

    comp[...] = jnp.zeros(comp.shape, BF16)
    row_i = lax.broadcasted_iota(jnp.int32, (256, 256), 0) // HEAD_DIM
    col_i = lax.broadcasted_iota(jnp.int32, (256, 256), 1) // HEAD_DIM
    ones_blk[...] = jnp.where(row_i == col_i, 1.0 / HEAD_DIM, 0.0).astype(BF16)

    half = (TR + 2 * HALO) * cols
    lane = lax.broadcasted_iota(jnp.int32, (1, half), 1)
    key_row = lane // cols
    key_col = lane % cols
    qi = lax.broadcasted_iota(jnp.int32, (TR * cols, 1), 0)
    row_off = key_row - qi // cols
    col_off = key_col - qi % cols
    for load in loads[1:6]:
        load.wait()
    near = (row_off >= 0) & (row_off <= 2 * HALO) & (col_off >= -HALO) & (col_off <= HALO)
    base = jnp.where(near, 1.0, 0.0).astype(F32)
    has_up = jnp.where(lat > 0, 1.0, 0.0).astype(F32)
    has_down = jnp.where(lat < n_lat - 1, 1.0, 0.0).astype(F32)

    def real_rows(key_row, top, count):
        ok = jnp.ones(key_row.shape, F32)
        for r in range(count):
            e = top + r
            if e < HALO:
                v = has_up
            elif e >= HALO + rows:
                v = has_down
            else:
                v = valid[e - HALO].astype(F32)
            ok = jnp.where(key_row == r, v, ok)
        return ok

    for slot, tile in enumerate((0, 1, 2, None, tiles - 3, tiles - 2, tiles - 1)):
        m = base if tile is None else base * real_rows(key_row, tile * TR, TR + 2 * HALO)
        masks[slot] = m.astype(BF16)

    supers = rows // SR
    side = 256
    s_lane = lax.broadcasted_iota(jnp.int32, (1, side), 1)
    s_row = s_lane // SIDE
    si = lax.broadcasted_iota(jnp.int32, (SR * SIDE, 1), 0)
    s_off = s_row - si // SIDE
    for which, q_col, k_col in ((0, si % SIDE, s_lane % SIDE - SIDE), (1, si % SIDE + cols - SIDE, s_lane % SIDE + cols)):
        c_off = k_col - q_col
        near = (s_off >= 0) & (s_off <= 2 * HALO) & (c_off >= -HALO) & (c_off <= HALO)
        base = jnp.where(near, 1.0, 0.0).astype(F32)
        for slot, sup in enumerate((0, None, supers - 1)):
            m = base if sup is None else base * real_rows(s_row, sup * SR, SR + 2 * HALO)
            smasks[2 * slot + which] = m.astype(BF16)

    enc_v = enc[...]
    wg_hi, wg_lo = split(enc_v.astype(F32) * gain[...])

    def put(x, at):
        hi, lo = split(x)
        comp[0 : x.shape[0], at : at + x.shape[1]] = hi
        comp[128 : 128 + x.shape[0], at : at + x.shape[1]] = lo

    put(nt(enc_v, enc_v) * (1.0 / enc_v.shape[1]), 2 * hd)
    for load, w, at in ((loads[6], wk, 0), (loads[7], wv, hd), (loads[8], wq, 2 * hd + 128)):
        load.wait()
        put(nn(wg_hi, w[...]) + nn(wg_lo, w[...]), at)

    def tiled(g):
        pair = jnp.concatenate([g[...]] * 2, axis=1)
        return jnp.concatenate([pair] * (hd // 128), axis=1)

    kg = tiled(k_gain)
    qg = tiled(q_gain) * (math.log2(math.e) / math.sqrt(HEAD_DIM))

    def head_norm(x, eps_u, g):
        sq = (x * x).astype(BF16)
        blk = ones_blk[...]
        mean = jnp.concatenate([nn(sq[:, i : i + 256], blk) for i in range(0, hd, 256)], axis=1)
        return x * lax.rsqrt(mean + eps_u) * g

    def project(f, k_ref, v_ref, at, q_at=None):
        n = f.shape[0]
        two = jnp.concatenate([f, f], axis=1)
        width = 2 * hd + 128 + (hd if q_at is not None else 0)
        y = nn(two, comp[:, 0:width])
        quad = jnp.sum(y[:, 2 * hd : 2 * hd + 128] * f.astype(F32), axis=1, keepdims=True)
        u = jnp.maximum(quad, 0.0) + EPS_ROW
        eps_u = EPS_HEAD * u
        k_ref[pl.ds(at, n), :] = head_norm(y[:, 0:hd], eps_u, kg).astype(BF16)
        v_ref[pl.ds(at, n), :] = (y[:, hd : 2 * hd] * lax.rsqrt(u)).astype(BF16)
        if q_at is not None:
            q = head_norm(y[:, 2 * hd + 128 :], eps_u, qg)
            q_s[pl.ds(q_at, n), :] = q.astype(BF16)
            q = q.reshape(n // cols, cols, hd)
            h_at = pl.ds(pl.multiple_of(q_at // 2, 16), n // 2)
            q_l[h_at, :] = q[:, 0:SIDE].reshape(n // 2, hd).astype(BF16)
            q_r[h_at, :] = q[:, cols - SIDE :].reshape(n // 2, hd).astype(BF16)

    crow = chunk_of(rows, 16)
    ccell = crow * cols

    def own_step(i, c):
        f = fext[pl.ds(HALO + i * crow, crow)].reshape(ccell, 128)
        project(f, k_o, v_o, pl.multiple_of(HALO * cols + i * ccell, 16), pl.multiple_of(i * ccell, 16))
        return c

    lax.fori_loop(0, rows // crow, own_step, 0, unroll=8)

    @pl.when(early)
    def _():
        meet()
        for copy in copies[2:]:
            copy.start()

    nq = TR * cols
    head = lax.broadcasted_iota(jnp.int32, (SR * SIDE, 256), 1) // HEAD_DIM

    def partial(q, k, v, m):
        n = q.shape[0]
        lanes = head[0:n]

        def pick(x):
            y = x[0:n]
            for h in range(1, 4):
                y = jnp.where(lanes == h, x[h * n : (h + 1) * n], y)
            return y

        zero = jnp.zeros_like(q)
        q4 = jnp.concatenate([jnp.where(lanes == h, q, zero) for h in range(4)], axis=0)
        e = jnp.exp2(nt(q4, k)).astype(BF16) * jnp.concatenate([m] * 4, axis=0)
        den = jnp.sum(e.astype(F32), axis=1, keepdims=True)
        return pick(nn(e, v)), pick(den)

    def own_part(t, c):
        o_at = pl.ds(pl.multiple_of(t * nq, nq), half)
        q_at = pl.ds(pl.multiple_of(t * nq, nq), nq)
        h_at = pl.ds(pl.multiple_of(t * (nq // 2), nq // 2), nq // 2)
        slot = jnp.minimum(t, 3) + jnp.maximum(t - (tiles - 4), 0)
        for p in range(hd // 256):
            ps = slice(256 * p, 256 * p + 256)
            num, den = partial(q_s[q_at, ps], k_o[o_at, ps], v_o[o_at, ps], masks[slot])
            for x, left_ref, right_ref in ((num, num_l, num_r), (den, den_l, den_r)):
                x = x.reshape(TR, cols, 256)
                left_ref[h_at, ps] = x[:, 0:SIDE].reshape(nq // 2, 256)
                right_ref[h_at, ps] = x[:, cols - SIDE :].reshape(nq // 2, 256)
        return c

    def side_part(u, c):
        ns = SR * SIDE
        q_at = pl.ds(pl.multiple_of(u * ns, ns), ns)
        s_at = pl.ds(pl.multiple_of(u * ns, ns), side)
        slot = 2 * (jnp.minimum(u, 1) + jnp.maximum(u - (supers - 2), 0))
        for p in range(hd // 256):
            ps = slice(256 * p, 256 * p + 256)
            halves = []
            for which, q_ref, k_ref, v_ref, num_ref, den_ref in (
                (0, q_l, k_l, v_l, num_l, den_l), (1, q_r, k_r, v_r, num_r, den_r)
            ):
                num, den = partial(q_ref[q_at, ps], k_ref[s_at, ps], v_ref[s_at, ps], smasks[slot + which])
                got = (num_ref[q_at, ps] + num) / (den_ref[q_at, ps] + den)
                halves.append(got.reshape(SR, SIDE, 256))
            both = jnp.concatenate(halves, axis=1).reshape(SR * cols, 256)
            mix[pl.ds(pl.multiple_of(u * SR * cols, SR * cols), SR * cols), ps] = both.astype(BF16)
        return c

    edge = -(-HALO // TR)
    lax.fori_loop(edge, tiles - edge, own_part, 0, unroll=chunk_of(tiles - 2 * edge, 7))

    for copy in copies:
        copy.wait_recv()

    for r0 in (0, HALO + rows):
        project(fext[r0 : r0 + HALO].reshape(HALO * cols, 128), k_o, v_o, r0 * cols)
    for t in (*range(edge), *range(tiles - edge, tiles)):
        own_part(t, 0)

    lead = HALO * SIDE
    pad = jnp.zeros((128 - deep, rows), F32)
    for halo, x_ref, up_ref, down_ref, at, slot in (
        (halo_l, x_l, c_ul, c_dl, cols - SIDE, SIDE - HALO), (halo_r, x_r, c_ur, c_dr, 0, 0)
    ):
        x_ref[0:lead, :] = up_ref[...].astype(F32)[:, at : at + SIDE].reshape(lead, 128)
        x_ref[lead + rows * SIDE : ext * SIDE, :] = down_ref[...].astype(F32)[:, at : at + SIDE].reshape(lead, 128)
        for c in range(HALO):
            block = jnp.concatenate([halo[c].astype(F32), pad], axis=0)
            x_ref[pl.ds(lead + slot + c, rows, stride=SIDE), :] = block.T

    total = x_l.shape[0]
    cside = chunk_of(total // 16, 14) * 16

    def side_step(i, c):
        for x_ref, k_ref, v_ref in ((x_l, k_l, v_l), (x_r, k_r, v_r)):
            at = pl.multiple_of(i * cside, 16)
            project(x_ref[pl.ds(at, cside), :].astype(BF16), k_ref, v_ref, at)
        return c

    lax.fori_loop(0, total // cside, side_step, 0, unroll=6)

    lax.fori_loop(0, supers, side_part, 0, unroll=SUNROLL)

    for copy in copies:
        copy.wait_send()
    to_hbm.wait()


def out_kernel(fields, w_enc, mix, w_out, out):
    f = fields[...]
    n = f.shape[0] * f.shape[1]
    latents = nn(f.reshape(n, f.shape[2])[:, 0 : w_enc.shape[0]], w_enc[...]).astype(BF16)
    res = latents.astype(F32) + nn(mix[...], w_out[...])
    out[...] = res.astype(BF16).reshape(out.shape)


def per_device(n_lat, n_lon, fields, row_valid, w_encode, norm_gain, w_query, w_key, w_value, query_gain, key_gain, w_out):
    rows, cols, chan = fields.shape
    d, hd = w_query.shape
    cells = rows * cols
    ext = rows + 2 * HALO
    fields_t = jnp.transpose(fields, (2, 1, 0))
    deep = -(-chan // 16) * 16
    hbm = pl.BlockSpec(memory_space=pltpu.HBM)
    vmem = pl.BlockSpec(memory_space=pltpu.VMEM)
    keys = (TR + 2 * HALO) * cols
    side_cells = (rows - SR) * SIDE + 256
    mix, by_cell = pl.pallas_call(
        functools.partial(attend_kernel, n_lat, n_lon, rows, cols, chan, hd),
        out_shape=(jax.ShapeDtypeStruct((cells, hd), BF16), jax.ShapeDtypeStruct((rows, cols, 128), BF16)),
        in_specs=[hbm] * 9,
        out_specs=(vmem, hbm),
        scratch_shapes=[
            pltpu.VMEM((cells // 2, hd), F32),
            pltpu.VMEM((cells // 2, hd), F32),
            pltpu.VMEM((cells // 2, hd), F32),
            pltpu.VMEM((cells // 2, hd), F32),
            pltpu.VMEM((cells // 2, hd), BF16),
            pltpu.VMEM((cells // 2, hd), BF16),
            pltpu.VMEM((6, SR * SIDE, 256), BF16),
            pltpu.VMEM((chan, cols, rows), BF16),
            pltpu.VMEM((128 * cols, rows), F32),
            pltpu.VMEM((cells, 128), F32),
            pltpu.VMEM((side_cells, 128), F32),
            pltpu.VMEM((side_cells, 128), F32),
            pltpu.VMEM((HALO, cols, 128), BF16),
            pltpu.VMEM((HALO, cols, 128), BF16),
            pltpu.VMEM((HALO, cols, 128), BF16),
            pltpu.VMEM((HALO, cols, 128), BF16),
            pltpu.VMEM((ext, cols, 128), BF16),
            pltpu.VMEM((HALO, deep, rows), BF16),
            pltpu.VMEM((HALO, deep, rows), BF16),
            pltpu.VMEM((HALO, deep, rows), BF16),
            pltpu.VMEM((HALO, deep, rows), BF16),
            pltpu.VMEM((chan, d), BF16),
            pltpu.VMEM((1, d), F32),
            pltpu.VMEM((d, hd), BF16),
            pltpu.VMEM((d, hd), BF16),
            pltpu.VMEM((d, hd), BF16),
            pltpu.VMEM((1, HEAD_DIM), F32),
            pltpu.VMEM((1, HEAD_DIM), F32),
            pltpu.SMEM((rows,), jnp.int32),
            pltpu.VMEM((256, 3 * hd + 128), BF16),
            pltpu.VMEM((256, 256), BF16),
            pltpu.VMEM((cells, hd), BF16),
            pltpu.VMEM((ext * cols, hd), BF16),
            pltpu.VMEM((ext * cols, hd), BF16),
            pltpu.VMEM((side_cells, hd), BF16),
            pltpu.VMEM((side_cells, hd), BF16),
            pltpu.VMEM((side_cells, hd), BF16),
            pltpu.VMEM((side_cells, hd), BF16),
            pltpu.VMEM((7, TR * cols, keys), BF16),
            pltpu.SemaphoreType.DMA((9,)),
            pltpu.SemaphoreType.DMA((8,)),
            pltpu.SemaphoreType.DMA((8,)),
            pltpu.SemaphoreType.DMA,
        ],
        compiler_params=pltpu.CompilerParams(
            collective_id=0, has_side_effects=True, vmem_limit_bytes=63 * 1024 * 1024
        ),
    )(
        fields_t, row_valid, w_encode, norm_gain.reshape(1, d), w_query, w_key, w_value,
        query_gain.reshape(1, HEAD_DIM), key_gain.reshape(1, HEAD_DIM),
    )
    block = chunk_of(rows, 32)
    return pl.pallas_call(
        out_kernel,
        grid=(rows // block,),
        out_shape=jax.ShapeDtypeStruct((rows, cols, d), BF16),
        in_specs=[
            pl.BlockSpec((block, cols, 128), lambda i: (i, 0, 0)),
            pl.BlockSpec((chan, d), lambda i: (0, 0)),
            pl.BlockSpec((block * cols, hd), lambda i: (i, 0)),
            pl.BlockSpec((hd, d), lambda i: (0, 0)),
        ],
        out_specs=pl.BlockSpec((block, cols, d), lambda i: (i, 0, 0)),
        compiler_params=pltpu.CompilerParams(vmem_limit_bytes=63 * 1024 * 1024),
    )(by_cell, w_encode, mix, w_out)


def solution(mesh):
    return jax.shard_map(
        functools.partial(per_device, mesh.shape["lat"], mesh.shape["lon"]),
        mesh=mesh,
        in_specs=(P("lat", "lon", None), P("lat"), P(), P(), P(), P(), P(), P(), P(), P()),
        out_specs=P("lat", "lon", None),
        check_vma=False,
    )
```

```python
import functools
import math

import jax
import jax.numpy as jnp
from jax import lax
from jax.experimental import pallas as pl
from jax.experimental.pallas import tpu as pltpu
from jax.sharding import PartitionSpec as P

HEADS = 8
HEAD_DIM = 64
HALO = 6
TR = 4
SR = 16
SIDE = 8
SUNROLL = 8
RING = 8
EPS_ROW = 1e-05
EPS_HEAD = 1e-06
F32 = jnp.float32
BF16 = jnp.bfloat16
MESH = pl.DeviceIdType.MESH
NT = (((1,), (1,)), ((), ()))


def nn(a, b):
    return jnp.dot(a, b, preferred_element_type=F32)


def nt(a, b):
    return lax.dot_general(a, b, NT, preferred_element_type=F32)


def split(x):
    hi = x.astype(BF16)
    return hi, (x - hi.astype(F32)).astype(BF16)


def chunk_of(count, most):
    return max(c for c in range(1, most + 1) if count % c == 0)


def attend_kernel(
    n_lat, n_lon, rows, cols, chan, hd,
    fields_t, row_valid, w_enc, norm_gain, w_q, w_k, w_v, query_gain, key_gain,
    mix, cells_out,
    num_l, num_r, den_l, den_r, q_l, q_r, smasks, ft, work, cell_f, x_l, x_r, c_ul, c_ur, c_dl, c_dr, fext, send_l, send_r, halo_l, halo_r, enc, gain, wq, wk, wv, q_gain, k_gain, valid, comp, ones_blk,
    q_s, k_o, v_o, k_l, v_l, k_r, v_r, masks,
    local_sem, send_sem, recv_sem, out_sem,
):
    lat, lon = lax.axis_index("lat"), lax.axis_index("lon")
    up, down = lax.rem(lat + n_lat - 1, n_lat), lax.rem(lat + 1, n_lat)
    left, right = lax.rem(lon + n_lon - 1, n_lon), lax.rem(lon + 1, n_lon)
    ext = rows + 2 * HALO
    tiles = rows // TR

    loads = [
        pltpu.make_async_copy(src, dst, local_sem.at[i])
        for i, (src, dst) in enumerate(
            (
                (fields_t, ft), (w_enc, enc), (norm_gain, gain), (row_valid, valid), (query_gain, q_gain),
                (key_gain, k_gain), (w_k, wk), (w_v, wv), (w_q, wq),
            )
        )
    ]
    for load in loads:
        load.start()

    barrier = pltpu.get_barrier_semaphore()
    around = [
        (up, left), (up, lon), (up, right), (lat, left), (lat, right), (down, left), (down, lon), (down, right)
    ]
    for dev in around:
        pl.semaphore_signal(barrier, inc=1, device_id=dev, device_id_type=MESH)

    work[chan * cols :, :] = jnp.zeros((work.shape[0] - chan * cols, rows), F32)
    x_l[...] = jnp.zeros(x_l.shape, F32)
    x_r[...] = jnp.zeros(x_r.shape, F32)
    loads[0].wait()
    work[0 : chan * cols, :] = ft[...].astype(F32).reshape(chan * cols, rows)
    deep = send_l.shape[1]
    for c in range(HALO):
        send_l[c] = work[pl.ds(c, deep, stride=cols), :].astype(BF16)
        send_r[c] = work[pl.ds(cols - HALO + c, deep, stride=cols), :].astype(BF16)

    head_rows, tail_rows = pl.ds(HALO, HALO), pl.ds(rows, HALO)
    above, below = pl.ds(0, HALO), pl.ds(HALO + rows, HALO)
    plan = [
        (send_l.at[...], halo_r.at[...], (lat, left)),
        (send_r.at[...], halo_l.at[...], (lat, right)),
        (fext.at[head_rows], fext.at[below], (up, lon)),
        (fext.at[tail_rows], fext.at[above], (down, lon)),
        (fext.at[head_rows], c_dr.at[...], (up, left)),
        (fext.at[tail_rows], c_ur.at[...], (down, left)),
        (fext.at[head_rows], c_dl.at[...], (up, right)),
        (fext.at[tail_rows], c_ul.at[...], (down, right)),
    ]
    copies = [
        pltpu.make_async_remote_copy(
            src_ref=src, dst_ref=dst, send_sem=send_sem.at[i], recv_sem=recv_sem.at[i],
            device_id=dev, device_id_type=MESH,
        )
        for i, (src, dst, dev) in enumerate(plan)
    ]

    early = lax.rem(lon, RING) == 0

    def meet():
        pl.semaphore_wait(barrier, 8)
        for copy in copies[:2]:
            copy.start()

    @pl.when(jnp.logical_not(early))
    def _():
        meet()

    for c in range(cols):
        cell_f[pl.ds(c, rows, stride=cols), :] = work[pl.ds(c, 128, stride=cols), :].T
    fext[pl.ds(HALO, rows)] = cell_f[...].astype(BF16).reshape(rows, cols, 128)
    to_hbm = pltpu.make_async_copy(fext.at[pl.ds(HALO, rows)], cells_out, out_sem)
    to_hbm.start()

    @pl.when(jnp.logical_not(early))
    def _():
        for copy in copies[2:]:
            copy.start()

    comp[...] = jnp.zeros(comp.shape, BF16)
    row_i = lax.broadcasted_iota(jnp.int32, (256, 256), 0) // HEAD_DIM
    col_i = lax.broadcasted_iota(jnp.int32, (256, 256), 1) // HEAD_DIM
    ones_blk[...] = jnp.where(row_i == col_i, 1.0 / HEAD_DIM, 0.0).astype(BF16)

    half = (TR + 2 * HALO) * cols
    lane = lax.broadcasted_iota(jnp.int32, (1, half), 1)
    key_row = lane // cols
    key_col = lane % cols
    qi = lax.broadcasted_iota(jnp.int32, (TR * cols, 1), 0)
    row_off = key_row - qi // cols
    col_off = key_col - qi % cols
    for load in loads[1:6]:
        load.wait()
    near = (row_off >= 0) & (row_off <= 2 * HALO) & (col_off >= -HALO) & (col_off <= HALO)
    base = jnp.where(near, 1.0, 0.0).astype(F32)
    has_up = jnp.where(lat > 0, 1.0, 0.0).astype(F32)
    has_down = jnp.where(lat < n_lat - 1, 1.0, 0.0).astype(F32)

    def real_rows(key_row, top, count):
        ok = jnp.ones(key_row.shape, F32)
        for r in range(count):
            e = top + r
            if e < HALO:
                v = has_up
            elif e >= HALO + rows:
                v = has_down
            else:
                v = valid[e - HALO].astype(F32)
            ok = jnp.where(key_row == r, v, ok)
        return ok

    for slot, tile in enumerate((0, 1, 2, None, tiles - 3, tiles - 2, tiles - 1)):
        m = base if tile is None else base * real_rows(key_row, tile * TR, TR + 2 * HALO)
        masks[slot] = m.astype(BF16)

    supers = rows // SR
    side = 256
    s_lane = lax.broadcasted_iota(jnp.int32, (1, side), 1)
    s_row = s_lane // SIDE
    si = lax.broadcasted_iota(jnp.int32, (SR * SIDE, 1), 0)
    s_off = s_row - si // SIDE
    for which, q_col, k_col in ((0, si % SIDE, s_lane % SIDE - SIDE), (1, si % SIDE + cols - SIDE, s_lane % SIDE + cols)):
        c_off = k_col - q_col
        near = (s_off >= 0) & (s_off <= 2 * HALO) & (c_off >= -HALO) & (c_off <= HALO)
        base = jnp.where(near, 1.0, 0.0).astype(F32)
        for slot, sup in enumerate((0, None, supers - 1)):
            m = base if sup is None else base * real_rows(s_row, sup * SR, SR + 2 * HALO)
            smasks[2 * slot + which] = m.astype(BF16)

    enc_v = enc[...]
    wg_hi, wg_lo = split(enc_v.astype(F32) * gain[...])

    def put(x, at):
        hi, lo = split(x)
        comp[0 : x.shape[0], at : at + x.shape[1]] = hi
        comp[128 : 128 + x.shape[0], at : at + x.shape[1]] = lo

    put(nt(enc_v, enc_v) * (1.0 / enc_v.shape[1]), 2 * hd)
    for load, w, at in ((loads[6], wk, 0), (loads[7], wv, hd), (loads[8], wq, 2 * hd + 128)):
        load.wait()
        put(nn(wg_hi, w[...]) + nn(wg_lo, w[...]), at)

    def tiled(g):
        pair = jnp.concatenate([g[...]] * 2, axis=1)
        return jnp.concatenate([pair] * (hd // 128), axis=1)

    kg = tiled(k_gain)
    qg = tiled(q_gain) * (math.log2(math.e) / math.sqrt(HEAD_DIM))

    def head_norm(x, eps_u, g):
        sq = (x * x).astype(BF16)
        blk = ones_blk[...]
        mean = jnp.concatenate([nn(sq[:, i : i + 256], blk) for i in range(0, hd, 256)], axis=1)
        return x * lax.rsqrt(mean + eps_u) * g

    def project(f, k_ref, v_ref, at, q_at=None):
        n = f.shape[0]
        two = jnp.concatenate([f, f], axis=1)
        width = 2 * hd + 128 + (hd if q_at is not None else 0)
        y = nn(two, comp[:, 0:width])
        quad = jnp.sum(y[:, 2 * hd : 2 * hd + 128] * f.astype(F32), axis=1, keepdims=True)
        u = jnp.maximum(quad, 0.0) + EPS_ROW
        eps_u = EPS_HEAD * u
        k_ref[pl.ds(at, n), :] = head_norm(y[:, 0:hd], eps_u, kg).astype(BF16)
        v_ref[pl.ds(at, n), :] = (y[:, hd : 2 * hd] * lax.rsqrt(u)).astype(BF16)
        if q_at is not None:
            q = head_norm(y[:, 2 * hd + 128 :], eps_u, qg)
            q_s[pl.ds(q_at, n), :] = q.astype(BF16)
            q = q.reshape(n // cols, cols, hd)
            h_at = pl.ds(pl.multiple_of(q_at // 2, 16), n // 2)
            q_l[h_at, :] = q[:, 0:SIDE].reshape(n // 2, hd).astype(BF16)
            q_r[h_at, :] = q[:, cols - SIDE :].reshape(n // 2, hd).astype(BF16)

    crow = chunk_of(rows, 16)
    ccell = crow * cols

    def own_step(i, c):
        f = fext[pl.ds(HALO + i * crow, crow)].reshape(ccell, 128)
        project(f, k_o, v_o, pl.multiple_of(HALO * cols + i * ccell, 16), pl.multiple_of(i * ccell, 16))
        return c

    lax.fori_loop(0, rows // crow, own_step, 0, unroll=8)

    @pl.when(early)
    def _():
        meet()
        for copy in copies[2:]:
            copy.start()

    nq = TR * cols
    head = lax.broadcasted_iota(jnp.int32, (SR * SIDE, 256), 1) // HEAD_DIM

    def partial(q, k, v, m):
        n = q.shape[0]
        lanes = head[0:n]

        def pick(x):
            y = x[0:n]
            for h in range(1, 4):
                y = jnp.where(lanes == h, x[h * n : (h + 1) * n], y)
            return y

        zero = jnp.zeros_like(q)
        q4 = jnp.concatenate([jnp.where(lanes == h, q, zero) for h in range(4)], axis=0)
        e = jnp.exp2(nt(q4, k)).astype(BF16) * jnp.concatenate([m] * 4, axis=0)
        den = jnp.sum(e.astype(F32), axis=1, keepdims=True)
        return pick(nn(e, v)), pick(den)

    def own_part(t, c):
        o_at = pl.ds(pl.multiple_of(t * nq, nq), half)
        q_at = pl.ds(pl.multiple_of(t * nq, nq), nq)
        h_at = pl.ds(pl.multiple_of(t * (nq // 2), nq // 2), nq // 2)
        slot = jnp.minimum(t, 3) + jnp.maximum(t - (tiles - 4), 0)
        for p in range(hd // 256):
            ps = slice(256 * p, 256 * p + 256)
            num, den = partial(q_s[q_at, ps], k_o[o_at, ps], v_o[o_at, ps], masks[slot])
            for x, left_ref, right_ref in ((num, num_l, num_r), (den, den_l, den_r)):
                x = x.reshape(TR, cols, 256)
                left_ref[h_at, ps] = x[:, 0:SIDE].reshape(nq // 2, 256)
                right_ref[h_at, ps] = x[:, cols - SIDE :].reshape(nq // 2, 256)
        return c

    def side_half(u, p, which, q_ref, k_ref, v_ref, num_ref, den_ref):
        ns = SR * SIDE
        ps = slice(256 * p, 256 * p + 256)
        q_at = pl.ds(pl.multiple_of(u * ns, ns), ns)
        s_at = pl.ds(pl.multiple_of(u * ns, ns), side)
        slot = 2 * (jnp.minimum(u, 1) + jnp.maximum(u - (supers - 2), 0)) + which
        num, den = partial(q_ref[q_at, ps], k_ref[s_at, ps], v_ref[s_at, ps], smasks[slot])
        return q_at, ps, (num_ref[q_at, ps] + num) / (den_ref[q_at, ps] + den)

    def right_part(u, c):
        for p in range(hd // 256):
            q_at, ps, got = side_half(u, p, 1, q_r, k_r, v_r, num_r, den_r)
            num_r[q_at, ps] = got
        return c

    def left_part(u, c):
        for p in range(hd // 256):
            q_at, ps, got = side_half(u, p, 0, q_l, k_l, v_l, num_l, den_l)
            both = [x.reshape(SR, SIDE, 256) for x in (got, num_r[q_at, ps])]
            both = jnp.concatenate(both, axis=1).reshape(SR * cols, 256)
            mix[pl.ds(pl.multiple_of(u * SR * cols, SR * cols), SR * cols), ps] = both.astype(BF16)
        return c

    edge = -(-HALO // TR)
    lax.fori_loop(edge, tiles - edge, own_part, 0, unroll=chunk_of(tiles - 2 * edge, 7))

    for i in (2, 3):
        copies[i].wait_recv()

    for r0 in (0, HALO + rows):
        project(fext[r0 : r0 + HALO].reshape(HALO * cols, 128), k_o, v_o, r0 * cols)
    for t in (*range(edge), *range(tiles - edge, tiles)):
        own_part(t, 0)

    lead = HALO * SIDE
    pad = jnp.zeros((128 - deep, rows), F32)
    total = x_l.shape[0]
    cside = chunk_of(total // 16, 14) * 16
    for arrivals, halo, x_ref, k_ref, v_ref, up_ref, down_ref, at, slot, part in (
        ((0, 4, 5), halo_r, x_r, k_r, v_r, c_ur, c_dr, 0, 0, right_part),
        ((1, 6, 7), halo_l, x_l, k_l, v_l, c_ul, c_dl, cols - SIDE, SIDE - HALO, left_part),
    ):
        for i in arrivals:
            copies[i].wait_recv()
        x_ref[0:lead, :] = up_ref[...].astype(F32)[:, at : at + SIDE].reshape(lead, 128)
        x_ref[lead + rows * SIDE : ext * SIDE, :] = down_ref[...].astype(F32)[:, at : at + SIDE].reshape(lead, 128)
        for c in range(HALO):
            block = jnp.concatenate([halo[c].astype(F32), pad], axis=0)
            x_ref[pl.ds(lead + slot + c, rows, stride=SIDE), :] = block.T

        def side_step(i, c):
            at = pl.multiple_of(i * cside, 16)
            project(x_ref[pl.ds(at, cside), :].astype(BF16), k_ref, v_ref, at)
            return c

        lax.fori_loop(0, total // cside, side_step, 0, unroll=6)
        lax.fori_loop(0, supers, part, 0, unroll=SUNROLL)

    for copy in copies:
        copy.wait_send()
    to_hbm.wait()


def out_kernel(fields, w_enc, mix, w_out, out):
    f = fields[...]
    n = f.shape[0] * f.shape[1]
    latents = nn(f.reshape(n, f.shape[2])[:, 0 : w_enc.shape[0]], w_enc[...]).astype(BF16)
    res = latents.astype(F32) + nn(mix[...], w_out[...])
    out[...] = res.astype(BF16).reshape(out.shape)


def per_device(n_lat, n_lon, fields, row_valid, w_encode, norm_gain, w_query, w_key, w_value, query_gain, key_gain, w_out):
    rows, cols, chan = fields.shape
    d, hd = w_query.shape
    cells = rows * cols
    ext = rows + 2 * HALO
    fields_t = jnp.transpose(fields, (2, 1, 0))
    deep = -(-chan // 16) * 16
    hbm = pl.BlockSpec(memory_space=pltpu.HBM)
    vmem = pl.BlockSpec(memory_space=pltpu.VMEM)
    keys = (TR + 2 * HALO) * cols
    side_cells = (rows - SR) * SIDE + 256
    mix, by_cell = pl.pallas_call(
        functools.partial(attend_kernel, n_lat, n_lon, rows, cols, chan, hd),
        out_shape=(jax.ShapeDtypeStruct((cells, hd), BF16), jax.ShapeDtypeStruct((rows, cols, 128), BF16)),
        in_specs=[hbm] * 9,
        out_specs=(vmem, hbm),
        scratch_shapes=[
            pltpu.VMEM((cells // 2, hd), F32),
            pltpu.VMEM((cells // 2, hd), F32),
            pltpu.VMEM((cells // 2, hd), F32),
            pltpu.VMEM((cells // 2, hd), F32),
            pltpu.VMEM((cells // 2, hd), BF16),
            pltpu.VMEM((cells // 2, hd), BF16),
            pltpu.VMEM((6, SR * SIDE, 256), BF16),
            pltpu.VMEM((chan, cols, rows), BF16),
            pltpu.VMEM((128 * cols, rows), F32),
            pltpu.VMEM((cells, 128), F32),
            pltpu.VMEM((side_cells, 128), F32),
            pltpu.VMEM((side_cells, 128), F32),
            pltpu.VMEM((HALO, cols, 128), BF16),
            pltpu.VMEM((HALO, cols, 128), BF16),
            pltpu.VMEM((HALO, cols, 128), BF16),
            pltpu.VMEM((HALO, cols, 128), BF16),
            pltpu.VMEM((ext, cols, 128), BF16),
            pltpu.VMEM((HALO, deep, rows), BF16),
            pltpu.VMEM((HALO, deep, rows), BF16),
            pltpu.VMEM((HALO, deep, rows), BF16),
            pltpu.VMEM((HALO, deep, rows), BF16),
            pltpu.VMEM((chan, d), BF16),
            pltpu.VMEM((1, d), F32),
            pltpu.VMEM((d, hd), BF16),
            pltpu.VMEM((d, hd), BF16),
            pltpu.VMEM((d, hd), BF16),
            pltpu.VMEM((1, HEAD_DIM), F32),
            pltpu.VMEM((1, HEAD_DIM), F32),
            pltpu.SMEM((rows,), jnp.int32),
            pltpu.VMEM((256, 3 * hd + 128), BF16),
            pltpu.VMEM((256, 256), BF16),
            pltpu.VMEM((cells, hd), BF16),
            pltpu.VMEM((ext * cols, hd), BF16),
            pltpu.VMEM((ext * cols, hd), BF16),
            pltpu.VMEM((side_cells, hd), BF16),
            pltpu.VMEM((side_cells, hd), BF16),
            pltpu.VMEM((side_cells, hd), BF16),
            pltpu.VMEM((side_cells, hd), BF16),
            pltpu.VMEM((7, TR * cols, keys), BF16),
            pltpu.SemaphoreType.DMA((9,)),
            pltpu.SemaphoreType.DMA((8,)),
            pltpu.SemaphoreType.DMA((8,)),
            pltpu.SemaphoreType.DMA,
        ],
        compiler_params=pltpu.CompilerParams(
            collective_id=0, has_side_effects=True, vmem_limit_bytes=63 * 1024 * 1024
        ),
    )(
        fields_t, row_valid, w_encode, norm_gain.reshape(1, d), w_query, w_key, w_value,
        query_gain.reshape(1, HEAD_DIM), key_gain.reshape(1, HEAD_DIM),
    )
    block = chunk_of(rows, 32)
    return pl.pallas_call(
        out_kernel,
        grid=(rows // block,),
        out_shape=jax.ShapeDtypeStruct((rows, cols, d), BF16),
        in_specs=[
            pl.BlockSpec((block, cols, 128), lambda i: (i, 0, 0)),
            pl.BlockSpec((chan, d), lambda i: (0, 0)),
            pl.BlockSpec((block * cols, hd), lambda i: (i, 0)),
            pl.BlockSpec((hd, d), lambda i: (0, 0)),
        ],
        out_specs=pl.BlockSpec((block, cols, d), lambda i: (i, 0, 0)),
        compiler_params=pltpu.CompilerParams(vmem_limit_bytes=63 * 1024 * 1024),
    )(by_cell, w_encode, mix, w_out)


def solution(mesh):
    return jax.shard_map(
        functools.partial(per_device, mesh.shape["lat"], mesh.shape["lon"]),
        mesh=mesh,
        in_specs=(P("lat", "lon", None), P("lat"), P(), P(), P(), P(), P(), P(), P(), P()),
        out_specs=P("lat", "lon", None),
        check_vma=False,
    )
```
